32 devices in a mesh: space: 8 (over y, x, core), wave: 4 (over z).
Axes of the slice: x: 2, y: 2, z: 4, core: 2. Of those that a mesh axis runs over, the one named last changes fastest.
Arguments:
- noise: float32 [8, 3, 8192], P(None, None, 'space'), may hold values from -6 to 6
- positions: float32 [3, 8192], P(None, 'space'), may hold values from 0 to 8, as said below
- wave_index: int32 [3, 4096], P(None, 'wave'), may hold values from -16 to 16, as said below
- tile_lists: int32 [64, 8], P('space'), may hold values from 0 to 23, as said below
- tile_counts: int32 [64], P('space'), may hold values from 0 to 8, as said below
Outputs:
- displacement: float32 [8, 3, 8192], P(None, None, 'space')
The draws below stay inside these ranges and needn't reach their ends.
Inputs may be any that keep to these rules, and one draw needn't show every extreme that they name: `positions`: particle j has x between j // 1024 and j // 1024 + 1, and y and z between 0 and 8. `wave_index`: row 0 holds n_1 from 1 to 16; rows 1 and 2 hold values from -16 to 15. `tile_lists`: A tile's 8 entries are distinct; window indices below 8 name tiles of the slab before, the next 8 tiles of the own slab, the rest tiles of the slab after. `tile_counts`: the counts of the 8 tiles of one slab add up to exactly 32, and in every slab one tile has 8.
All inputs are finite; a program needn't handle non-finite values.
Results may differ from the reference program's by a relative error of at most 0.0003.
Values sent between devices are 32-bit elements; how exact they have to be, the bound alone decides.
No kernel may reach another device: no remote copies, remote signals or barrier semaphores. Data moves between devices by JAX's collectives and lax.ppermute only.
A program may use at most 64 MiB of HBM per device.

```python
import math
import jax
import jax.numpy as jnp
from jax import lax

NVEC = 8
P_BLK = 1024
TILE = 128
KW = 4096
NB_MOST = 8
DEGREE = 3
TILES = 8
TILES_ALL = 64
PAIR_MOST = 32
PARTICLES = 8192
N_SPACE = 8


def draw_positions(key, part):
    across = jax.random.uniform(jax.random.fold_in(key, 11), (PARTICLES,), jnp.float32)
    cross = jax.random.uniform(jax.random.fold_in(key, 12), (2, PARTICLES), jnp.float32)
    slab_start = (jnp.arange(PARTICLES) // P_BLK).astype(jnp.float32)
    return jnp.concatenate([(slab_start + across)[None, :], 8.0 * cross], axis=0).astype(jnp.float32)


def draw_wave_index(key, part):
    first_row = jax.random.randint(jax.random.fold_in(key, 21), (1, KW), 1, 17)
    other_rows = jax.random.randint(jax.random.fold_in(key, 22), (2, KW), -16, 16)
    return jnp.concatenate([first_row, other_rows], axis=0).astype(jnp.int32)


def draw_tile_lists(key, part):
    subkeys = jax.random.split(jax.random.fold_in(key, 31), TILES_ALL)

    def pick_window(subkey):
        return jax.random.permutation(subkey, 3 * TILES)[:NB_MOST]
    return jax.vmap(pick_window)(subkeys).astype(jnp.int32)


def draw_tile_counts(key, part):
    subkeys = jax.random.split(jax.random.fold_in(key, 41), TILES_ALL // TILES)

    def block_counts(subkey):
        full_tile = jax.random.randint(jax.random.fold_in(subkey, 1), (), 0, TILES)
        chosen = jax.random.permutation(jax.random.fold_in(subkey, 2), (TILES - 1) * NB_MOST)[:PAIR_MOST - NB_MOST]
        owner = chosen // NB_MOST
        others = jnp.sum((owner[:, None] == jnp.arange(TILES - 1)[None, :]).astype(jnp.int32), axis=0)
        index_ids = jnp.arange(TILES)
        shifted = jnp.clip(index_ids - (index_ids > full_tile).astype(jnp.int32), 0, TILES - 2)
        return jnp.where(index_ids == full_tile, NB_MOST, others[shifted]).astype(jnp.int32)
    return jax.vmap(block_counts)(subkeys).reshape(TILES_ALL).astype(jnp.int32)


def levels(key, shape, cuts, smallest, top_value):
    level = 1.0
    for axis_at, shards_of in cuts:
        heights = jax.random.uniform(jax.random.fold_in(jax.random.fold_in(key, 6), axis_at), (shards_of,), jnp.float32, smallest / len(cuts), top_value / len(cuts))
        level = level * jnp.repeat(jnp.exp(heights), shape[axis_at] // shards_of).reshape((-1,) + (1,) * (len(shape) - 1 - axis_at))
    return level


def scatter_about(own_key, shape, spread, reach, cuts=(), kind=jnp.bfloat16):
    values = jax.random.normal(own_key, shape, jnp.float32) * spread
    if len(cuts) > 0:
        values = levels(own_key, shape, cuts, -0.22, 0.18) * values
    return jnp.clip(values, min=-reach, max=reach).astype(kind)


def setup_inputs(seed: int = 0) -> dict:
    splits = jax.random.split(jax.random.key(seed), 6)
    return {
        "noise": scatter_about(splits[0], (NVEC, 3, PARTICLES), 1.0, 6.0, ((2, 8),), jnp.float32),
        "positions": draw_positions(jax.random.fold_in(splits[5], 71), 0),
        "wave_index": draw_wave_index(jax.random.fold_in(splits[5], 71), 0),
        "tile_lists": draw_tile_lists(jax.random.fold_in(splits[5], 71), 0),
        "tile_counts": draw_tile_counts(jax.random.fold_in(splits[5], 71), 0),
    }


PRECISE = lax.Precision.HIGHEST
SIDE_CROSS = 8.0
NEAR_SQUARE = 0.36
NEAR_AMP = 0.15
FAR_AMP = 8.0
SPLIT_SQUARE = 64.0
SCREEN = 4.0
SAFETY = 1.25
SPREAD = 100.0
EPSILON = 1e-06

def pair_block(target, source, self_flag, live_weight, length_x):
    box_sides = jnp.array([length_x, SIDE_CROSS, SIDE_CROSS], jnp.float32)[:, None, None]
    offset = target[:, None, :] - source[:, :, None]
    offset = offset - box_sides * jnp.floor(offset / box_sides + 0.5)
    distance_sq = lax.optimization_barrier(jnp.sum(offset * offset, axis=0))
    tile_width = target.shape[1]
    diagonal_mask = jnp.arange(tile_width)[:, None] == jnp.arange(tile_width)[None, :]
    keep_mask = jnp.where(diagonal_mask & self_flag, 0.0, 1.0) * live_weight
    envelope = NEAR_AMP * jnp.exp(-distance_sq / NEAR_SQUARE) * keep_mask
    outer_product = offset[None, :, :, :] * offset[:, None, :, :]
    identity = jnp.eye(3, dtype=jnp.float32)[:, :, None, None]
    pair_matrix = (identity + outer_product / NEAR_SQUARE) * envelope[None, None]
    return jnp.transpose(pair_matrix, (0, 2, 1, 3)).reshape(3 * tile_width, 3 * tile_width)

def wave_terms(indices, length_x):
    box_sides = jnp.array([length_x, SIDE_CROSS, SIDE_CROSS], jnp.float32)[:, None]
    wave_vectors = 2.0 * math.pi * indices.astype(jnp.float32) / box_sides
    wave_square = lax.optimization_barrier(jnp.sum(wave_vectors * wave_vectors, axis=0))
    scaled_square = wave_square / SPLIT_SQUARE
    weight = FAR_AMP * (1.0 + scaled_square) * jnp.exp(-scaled_square) / (KW * (wave_square + SCREEN))
    unit_waves = wave_vectors / jnp.sqrt(wave_square)
    return (wave_vectors, weight, unit_waves)

def make_phases(positions, wave_vectors):
    phase_angles = positions[0][:, None] * wave_vectors[0][None, :] + positions[1][:, None] * wave_vectors[1][None, :] + positions[2][:, None] * wave_vectors[2][None, :]
    return jnp.concatenate([jnp.cos(phase_angles), jnp.sin(phase_angles)], axis=1)

def project(factors, weight, unit_waves):
    along_wave = lax.optimization_barrier(jnp.sum(factors * unit_waves[None, :, None, :], axis=1))
    return weight * (factors - unit_waves[None, :, None, :] * along_wave[:, None])

def far_apply(forces, positions, wave_index):
    vectors = forces.shape[0]
    row_count = vectors * 3
    flattened = forces.reshape(row_count, forces.shape[2])
    wave_blocks = jnp.transpose(wave_index.reshape(3, KW // 512, 512), (1, 0, 2))

    def add_block(running_sum, indices):
        wave_vectors, weight, unit_waves = wave_terms(indices, float(N_SPACE))
        phases = make_phases(positions, wave_vectors)
        factors = jnp.dot(flattened, phases, precision=PRECISE, preferred_element_type=jnp.float32).reshape(vectors, 3, 2, 512)
        weighted = project(factors, weight, unit_waves).reshape(row_count, 1024)
        back = lax.dot_general(weighted, phases, (((1,), (1,)), ((), ())), precision=PRECISE, preferred_element_type=jnp.float32)
        return (running_sum + back, None)
    running_sum, _ = lax.scan(add_block, jnp.zeros((row_count, forces.shape[2]), jnp.float32), wave_blocks)
    return running_sum.reshape(forces.shape)

def near_apply(forces, positions, tile_lists, tile_counts):
    vectors = forces.shape[0]

    def one_tile(tile_id):
        slab_id = tile_id // TILES
        own_tile = tile_id % TILES
        target = lax.dynamic_slice_in_dim(positions, (tile_id * TILE).astype(jnp.int32), TILE, 1)

        def one_slot(slot_id):
            window = tile_lists[tile_id, slot_id]
            source_tile = ((slab_id - 1 + window // TILES) % N_SPACE * TILES + window % TILES).astype(jnp.int32)
            source = lax.dynamic_slice_in_dim(positions, source_tile * TILE, TILE, 1)
            pushed = lax.dynamic_slice_in_dim(forces, source_tile * TILE, TILE, 2).reshape(vectors, 3 * TILE)
            live_weight = jnp.where(slot_id < tile_counts[tile_id], 1.0, 0.0)
            matrix = pair_block(target, source, window == TILES + own_tile, live_weight, float(N_SPACE))
            return jnp.dot(pushed, matrix, precision=PRECISE, preferred_element_type=jnp.float32)
        slot_parts = jax.vmap(one_slot)(jnp.arange(NB_MOST, dtype=jnp.int32))
        return lax.optimization_barrier(jnp.sum(slot_parts, axis=0)).reshape(vectors, 3, TILE)
    pieces = lax.map(one_tile, jnp.arange(TILES_ALL, dtype=jnp.int32))
    return jnp.transpose(pieces, (1, 2, 0, 3)).reshape(forces.shape)

def chebyshev(lower_bound, upper_bound):
    node_count = DEGREE + 1
    node_angles = (jnp.arange(node_count, dtype=jnp.float32) + 0.5) * (math.pi / node_count)
    samples = jnp.sqrt(0.5 * (upper_bound - lower_bound) * jnp.cos(node_angles) + 0.5 * (upper_bound + lower_bound))
    orders = jnp.arange(node_count, dtype=jnp.float32)
    coeffs = 2.0 / node_count * lax.optimization_barrier(jnp.sum(samples[None, :] * jnp.cos(orders[:, None] * node_angles[None, :]), axis=1))
    return coeffs * jnp.where(orders == 0.0, 0.5, 1.0)

def reference(noise, positions, wave_index, tile_lists, tile_counts):

    def mobility(forces):
        return forces + near_apply(forces, positions, tile_lists, tile_counts) + far_apply(forces, positions, wave_index)
    first_image = mobility(noise)
    second = mobility(first_image)
    ratios = lax.optimization_barrier(jnp.sum(second * second, axis=(1, 2))) / (lax.optimization_barrier(jnp.sum(first_image * first_image, axis=(1, 2))) + EPSILON)
    upper_bound = SAFETY * jnp.sqrt(jnp.max(ratios))
    lower_bound = upper_bound / SPREAD
    coeffs = chebyshev(lower_bound, upper_bound)
    bound_sum = upper_bound + lower_bound
    bound_span = upper_bound - lower_bound
    previous = noise
    current = (2.0 * first_image - bound_sum * noise) / bound_span
    mapped = (2.0 * second - bound_sum * first_image) / bound_span
    running_sum = coeffs[0] * previous + coeffs[1] * current
    for degree_step in range(2, DEGREE + 1):
        following = 2.0 * (2.0 * mapped - bound_sum * current) / bound_span - previous
        running_sum = running_sum + coeffs[degree_step] * following
        if degree_step < DEGREE:
            mapped = mobility(following)
        previous, current = (current, following)
    return running_sum
```

```python
import functools
import math

import jax
import jax.numpy as jnp
from jax import lax
from jax.experimental import pallas as pl
from jax.experimental.pallas import tpu as pltpu
from jax.sharding import PartitionSpec as P

TILE = 128
KW = 4096
NB_MOST = 8
DEGREE = 3
PAIR_MOST = 32

SIDE_CROSS = 8.0
NEAR_SQUARE = 0.36
NEAR_AMP = 0.15
FAR_AMP = 8.0
SPLIT_SQUARE = 64.0
SCREEN = 4.0
SAFETY = 1.25
SPREAD = 100.0
EPSILON = 1e-06

F32 = jnp.float32
BF16 = jnp.bfloat16
VMEM_LIMIT = 24 << 20

SINE = (4.44287968, -7.30781651, 3.59777427, -0.791199386)
COSINE = (1.41421354, -6.97885084, 5.73946047, -1.88355792, 0.310688019)


def split(x):
    high = x.astype(BF16)
    return high, (x - high.astype(F32)).astype(BF16)


def poly(coeffs, x):
    acc = coeffs[-1]
    for c in coeffs[-2::-1]:
        acc = acc * x + c
    return acc


def forward(rows, cos_hi, sin_hi, cos_lo, sin_lo, terms, msg_ref):
    waves = cos_hi.shape[1]
    both = jnp.concatenate(split(rows), axis=0)
    high = both[:24]
    step = min(512, waves)
    for at in range(0, waves, step):
        cols = slice(at, at + step)
        pieces = []
        for hi_ref, lo_ref in ((cos_hi, cos_lo), (sin_hi, sin_lo)):
            first = jnp.dot(both, hi_ref[:, cols], preferred_element_type=F32)
            second = jnp.dot(high, lo_ref[:, cols], preferred_element_type=F32)
            full = first[:24] + (first[24:] + second)
            fx, fy, fz = full[0:8], full[8:16], full[16:24]
            t = terms[:, cols]
            pieces.append(t[1:2] * fx + t[2:3] * fy)
            pieces.append(t[3:4] * fx + t[4:5] * fy + t[5:6] * fz)
        stacked = jnp.concatenate(pieces, axis=0)
        for k in range(step // TILE):
            row = (at // TILE + k) * 32
            msg_ref[row : row + 32, :] = stacked[:, k * TILE : (k + 1) * TILE]


def start_kernel(
    length_x,
    pos_ref,
    noise_ref,
    index_ref,
    cos_hi,
    sin_hi,
    cos_lo,
    sin_lo,
    terms_ref,
    rows_ref,
    msg_ref,
    pack_ref,
    turn_ref,
):
    particles = pos_ref.shape[1]
    waves = index_ref.shape[1]
    tiles = particles // TILE
    sides = (length_x, SIDE_CROSS, SIDE_CROSS)
    counts = [index_ref[a : a + 1, :].astype(F32) for a in range(3)]
    k1, k2, k3 = [2.0 * math.pi * counts[a] / sides[a] for a in range(3)]
    square = k1 * k1 + k2 * k2 + k3 * k3
    scaled = square / SPLIT_SQUARE
    weight = FAR_AMP * (1.0 + scaled) * jnp.exp(-scaled) / (KW * (square + SCREEN))
    flat_square = k1 * k1 + k2 * k2
    flat = 1.0 / jnp.sqrt(flat_square)
    both = 1.0 / jnp.sqrt(square * flat_square)
    zero = jnp.zeros_like(k1)
    terms_ref[...] = jnp.concatenate(
        [weight, -k2 * flat, k1 * flat, -k1 * k3 * both, -k2 * k3 * both, flat_square * both, zero, zero],
        axis=0,
    )
    for a in range(3):
        rows_ref[8 * a : 8 * a + 8, :] = noise_ref[:, a, :]
    filler = jnp.zeros((5, TILE), F32)
    for i in range(tiles):
        lanes = slice(i * TILE, (i + 1) * TILE)
        pack_ref[32 * i : 32 * i + 24, :] = rows_ref[:, lanes]
        place = jnp.concatenate([pos_ref[:, lanes], filler], axis=0)
        pack_ref[32 * i + 24 : 32 * i + 32, :] = place
        for a in range(3):
            line = jnp.broadcast_to(place[a : a + 1] / sides[a], (TILE, TILE))
            turn_ref[a, i * TILE : (i + 1) * TILE, :] = line.T

    def block(at, carry):
        mine = pl.ds(pl.multiple_of(at * 16, 16), 16)
        u1, u2, u3 = [turn_ref[a, mine, :] for a in range(3)]
        for j in range(waves // TILE):
            cols = slice(j * TILE, (j + 1) * TILE)
            turns = u1 * counts[0][:, cols] + u2 * counts[1][:, cols] + u3 * counts[2][:, cols]
            r = turns - jnp.round(turns)
            x = r * r
            s = r * poly(SINE, x)
            c = poly(COSINE, x)
            cos_hi[mine, cols], cos_lo[mine, cols] = split(1.0 - s * s)
            sin_hi[mine, cols], sin_lo[mine, cols] = split(s * c)
        return carry

    lax.fori_loop(0, particles // 16, block, 0)
    forward(rows_ref[...], cos_hi, sin_hi, cos_lo, sin_lo, terms_ref[...], msg_ref)


def pair_kernel(
    length_x, share, meta_ref, lists_ref, counts_ref, own_ref, near_ref, away_ref, out_ref, plan_ref, place_ref
):
    tiles = lists_ref.shape[0]
    rank, ranks, odd = meta_ref[0], meta_ref[1], meta_ref[2]
    for p in range(share):
        for q in range(4):
            plan_ref[q, p] = 0

    def slot(at, seen):
        target, k = at // NB_MOST, at % NB_MOST
        live = k < counts_ref[target]
        at_p = seen // ranks

        @pl.when(live & (seen % ranks == rank) & (at_p < share))
        def _():
            window = lists_ref[target, k]
            side = window // tiles
            tile = window % tiles
            which = jnp.where(side == 1, 0, jnp.where((side == 0) == (odd == 1), 1, 2))
            plan_ref[0, at_p] = target
            plan_ref[1, at_p] = which * tiles + tile
            plan_ref[2, at_p] = jnp.where((side == 1) & (tile == target), 1, 0)
            plan_ref[3, at_p] = 1

        return seen + jnp.where(live, 1, 0)

    lax.fori_loop(0, tiles * NB_MOST, slot, 0)
    for slab, ref in enumerate((own_ref, near_ref, away_ref)):
        for i in range(tiles):
            place_ref[slab * tiles + i] = ref[32 * i + 24 : 32 * i + 32, :]
    sides = (length_x, SIDE_CROSS, SIDE_CROSS)
    off_diagonal = (
        lax.broadcasted_iota(jnp.int32, (TILE, TILE), 0) != lax.broadcasted_iota(jnp.int32, (TILE, TILE), 1)
    ).astype(F32)

    def pair(p, carry):
        target = place_ref[plan_ref[0, p]]
        source = place_ref[plan_ref[1, p]]
        own = plan_ref[2, p].astype(F32)
        keep = (1.0 - own * (1.0 - off_diagonal)) * plan_ref[3, p].astype(F32)
        d = []
        for a in range(3):
            line = jnp.broadcast_to(source[a : a + 1], (TILE, TILE)).T
            offset = target[a : a + 1] - line
            d.append(offset - sides[a] * jnp.floor(offset / sides[a] + 0.5))
        square = d[0] * d[0] + d[1] * d[1] + d[2] * d[2]
        envelope = NEAR_AMP * jnp.exp(-square / NEAR_SQUARE) * keep
        scaled = [envelope * d[a] * (1.0 / NEAR_SQUARE) for a in range(3)]
        at = 0
        for a in range(3):
            for b in range(a, 3):
                value = scaled[a] * d[b]
                if a == b:
                    value = value + envelope
                high, low = split(value)
                out_ref[p, 0:TILE, at * TILE : (at + 1) * TILE] = high
                out_ref[p, TILE : 2 * TILE, at * TILE : (at + 1) * TILE] = low
                at += 1
        return carry

    lax.fori_loop(0, share, pair, 0)


def near_kernel(stride, base, plan_ref, own_ref, near_ref, away_ref, pair_ref, out_ref, window_ref, sum_ref):
    tiles = sum_ref.shape[0]
    share = pair_ref.shape[0]
    for slab, ref in enumerate((own_ref, near_ref, away_ref)):
        for i in range(tiles):
            row = (base if slab < 2 else 0) + stride * i
            window_ref[slab * tiles + i] = ref[row : row + 24, :]
    sum_ref[...] = jnp.zeros_like(sum_ref)
    for p in range(share):
        target = plan_ref[0, p]
        high, low = split(window_ref[plan_ref[1, p]])
        left = jnp.concatenate(
            [jnp.concatenate([high, high], axis=1), jnp.concatenate([low, jnp.zeros_like(low)], axis=1)], axis=0
        )
        both = jnp.dot(left, pair_ref[p], preferred_element_type=F32)
        full = both[:24] + both[24:]
        x, y, z = full[0:8], full[8:16], full[16:24]

        def part(rows, at):
            return rows[:, at * TILE : (at + 1) * TILE]

        sum_ref[target] += jnp.concatenate(
            [
                part(x, 0) + part(y, 1) + part(z, 2),
                part(x, 1) + part(y, 3) + part(z, 4),
                part(x, 2) + part(y, 4) + part(z, 5),
            ],
            axis=0,
        )
    for i in range(tiles):
        out_ref[:, i * TILE : (i + 1) * TILE] = sum_ref[i]


def back_kernel(parts, *refs):
    ins, (terms_ref, cos_hi, sin_hi, cos_lo, sin_lo, near_ref, out_ref, norm_ref, left_ref) = (
        refs[:parts],
        refs[parts:],
    )
    waves = terms_ref.shape[1]
    particles = out_ref.shape[1]
    tiles = waves // TILE
    norm = ins[0][32 * tiles :, :]
    for ref in ins[1:]:
        norm = norm + ref[32 * tiles :, :]
    norm_ref[...] = norm
    for i in range(tiles):
        block = ins[0][32 * i : 32 * i + 32, :]
        for ref in ins[1:]:
            block = block + ref[32 * i : 32 * i + 32, :]
        t = terms_ref[:, i * TILE : (i + 1) * TILE]
        block = block * t[0:1]
        for kind in range(2):
            one, two = block[16 * kind : 16 * kind + 8], block[16 * kind + 8 : 16 * kind + 16]
            rows = jnp.concatenate(
                [t[1:2] * one + t[3:4] * two, t[2:3] * one + t[4:5] * two, t[5:6] * two], axis=0
            )
            left_ref[kind, :, i * TILE : (i + 1) * TILE] = jnp.concatenate(split(rows), axis=0)
    dims = (((1,), (1,)), ((), ()))
    step = min(256, particles)
    for at in range(0, particles, step):
        rows = slice(at, at + step)
        first = lax.dot_general(left_ref[0], cos_hi[rows, :], dims, preferred_element_type=F32)
        first += lax.dot_general(left_ref[1], sin_hi[rows, :], dims, preferred_element_type=F32)
        second = lax.dot_general(left_ref[0, 0:24], cos_lo[rows, :], dims, preferred_element_type=F32)
        second += lax.dot_general(left_ref[1, 0:24], sin_lo[rows, :], dims, preferred_element_type=F32)
        out_ref[:, rows] = first[:24] + (first[24:] + second) + near_ref[:, rows]


def step_kernel(parts, *refs):
    ins, (force_ref, terms_ref, cos_hi, sin_hi, cos_lo, sin_lo, rows_ref, msg_ref) = refs[:parts], refs[parts:]
    particles = force_ref.shape[1]
    waves = terms_ref.shape[1]
    total = ins[0][...]
    for ref in ins[1:]:
        total = total + ref[...]
    rows = force_ref[...] + total
    rows_ref[...] = rows
    squares = rows * rows
    squares = squares[0:8] + squares[8:16] + squares[16:24]
    tiles = particles // TILE
    norm = squares[:, 0:TILE]
    for i in range(1, tiles):
        norm = norm + squares[:, i * TILE : (i + 1) * TILE]
    base = waves // TILE * 32
    msg_ref[base : base + 8, :] = norm
    for i in range(tiles):
        msg_ref[base + 8 + 24 * i : base + 32 + 24 * i, :] = rows[:, i * TILE : (i + 1) * TILE]
    forward(rows, cos_hi, sin_hi, cos_lo, sin_lo, terms_ref[...], msg_ref)


def final_kernel(parts, *refs):
    ins, (noise_ref, one_ref, two_ref, first_ref, second_ref, out_ref) = refs[:parts], refs[parts:]
    total = ins[0][...]
    for ref in ins[1:]:
        total = total + ref[...]
    u0, u1, u2 = noise_ref[...], one_ref[...], two_ref[...]
    u3 = u2 + total
    first = jnp.sum(first_ref[...], axis=1, keepdims=True)
    second = jnp.sum(second_ref[...], axis=1, keepdims=True)
    ratio = jnp.max(second / (first + EPSILON), axis=0, keepdims=True)
    high = SAFETY * jnp.sqrt(ratio)
    low = high / SPREAD
    nodes = DEGREE + 1
    angles = [math.pi * (j + 0.5) / nodes for j in range(nodes)]
    samples = [jnp.sqrt(0.5 * (high - low) * math.cos(t) + 0.5 * (high + low)) for t in angles]
    coeffs = []
    for k in range(nodes):
        acc = samples[0] * math.cos(k * angles[0])
        for j in range(1, nodes):
            acc = acc + samples[j] * math.cos(k * angles[j])
        coeffs.append(acc * (2.0 / nodes) * (0.5 if k == 0 else 1.0))
    p = 2.0 / (high - low)
    q = (high + low) / (high - low)
    v0, v1, v2 = p * u1 - q * u0, p * u2 - q * u1, p * u3 - q * u2
    t2 = 2.0 * (p * v1 - q * v0) - u0
    m2 = 2.0 * (p * v2 - q * v1) - u1
    t3 = 2.0 * (p * m2 - q * t2) - v0
    out = coeffs[0] * u0 + coeffs[1] * v0 + coeffs[2] * t2 + coeffs[3] * t3
    for a in range(3):
        out_ref[:, a, :] = out[8 * a : 8 * a + 8]


def call(kernel, outs, args, scratch=(), smem_in=0, smem_out=()):
    vmem = pl.BlockSpec(memory_space=pltpu.VMEM)
    smem = pl.BlockSpec(memory_space=pltpu.SMEM)
    return pl.pallas_call(
        kernel,
        out_shape=[jax.ShapeDtypeStruct(*o) for o in outs],
        in_specs=[smem] * smem_in + [vmem] * (len(args) - smem_in),
        out_specs=[smem if i in smem_out else vmem for i in range(len(outs))],
        scratch_shapes=list(scratch),
        compiler_params=pltpu.CompilerParams(vmem_limit_bytes=VMEM_LIMIT),
    )(*args)


def exchange(x, axis, lowest):
    size = lax.axis_size(axis)
    bit = lowest
    parts = [x]
    while bit < size:
        if len(parts) > 1:
            x = functools.reduce(jnp.add, parts)
        radix = min(4, size // bit)
        parts = [x] + [
            lax.ppermute(x, axis, [(i, i ^ (d * bit)) for i in range(size)]) for d in range(1, radix)
        ]
        bit *= radix
    return parts


def body(noise, positions, wave_index, tile_lists, tile_counts):
    slabs, wave_count = lax.axis_size("space"), lax.axis_size("wave")
    length_x = float(slabs)
    vectors = noise.shape[0]
    particles = positions.shape[1]
    waves = wave_index.shape[1]
    tiles = particles // TILE
    share = PAIR_MOST // wave_count
    meta = jnp.stack(
        [lax.axis_index("wave"), jnp.int32(wave_count), lax.axis_index("space") % 2]
    ).astype(jnp.int32)
    core = [(i, i ^ 1) for i in range(slabs)]
    third = [(i, (i + 1 if i % 2 else i - 1) % slabs) for i in range(slabs)]
    table = ((particles, waves), BF16)
    rows_shape = ((3 * vectors, particles), F32)
    factor_rows = waves // TILE * 32

    cos_hi, sin_hi, cos_lo, sin_lo, terms, rows, msg, pack = call(
        functools.partial(start_kernel, length_x),
        [table] * 4 + [((8, waves), F32), rows_shape, ((factor_rows, TILE), F32), ((32 * tiles, TILE), F32)],
        (positions, noise, wave_index),
        [pltpu.VMEM((3, particles, TILE), F32)],
    )
    phases = (cos_hi, sin_hi, cos_lo, sin_lo)
    msg = jnp.concatenate([msg, jnp.zeros((8, TILE), F32), pack], axis=0)
    noise_rows = rows
    away = lax.ppermute(pack, "space", third)
    images, norms = [], []
    pairs = plan = None
    for step in range(DEGREE):
        other = lax.ppermute(msg, "space", core)
        chip = msg[: factor_rows + 8] + other[: factor_rows + 8]
        factors = exchange(chip, "space", 2)
        base, stride = factor_rows + 8, 32 if step == 0 else 24
        if step == 0:
            own, near = pack, other[base:]
            pairs, plan = call(
                functools.partial(pair_kernel, length_x, share),
                [((share, 2 * TILE, 6 * TILE), BF16), ((4, share), jnp.int32)],
                (meta, tile_lists, tile_counts, pack, other[base:], away),
                [pltpu.VMEM((3 * tiles, 8, TILE), F32)],
                smem_in=3,
                smem_out=(1,),
            )
        near_part = call(
            functools.partial(near_kernel, stride, base),
            [rows_shape],
            (plan, msg, other, away, pairs),
            [pltpu.VMEM((3 * tiles, 24, TILE), F32), pltpu.VMEM((tiles, 24, TILE), F32)],
            smem_in=1,
        )[0]
        part, norm = call(
            functools.partial(back_kernel, len(factors)),
            [rows_shape, ((8, TILE), F32)],
            (*factors, terms, *phases, near_part),
            [pltpu.VMEM((2, 48, waves), BF16)],
        )
        norms.append(norm)
        sums = exchange(part, "wave", 1)
        if step < DEGREE - 1:
            rows, msg = call(
                functools.partial(step_kernel, len(sums)),
                [rows_shape, ((factor_rows + 8 + 24 * tiles, TILE), F32)],
                (*sums, rows, terms, *phases),
            )
            images.append(rows)
            away = lax.ppermute(msg[factor_rows + 8 :], "space", third)
    return call(
        functools.partial(final_kernel, len(sums)),
        [((vectors, 3, particles), F32)],
        (*sums, noise_rows, *images, norms[1], norms[2]),
    )[0]


def solution(mesh):
    in_specs = (
        P(None, None, "space"),
        P(None, "space"),
        P(None, "wave"),
        P("space", None),
        P("space"),
    )
    out_specs = P(None, None, "space")
    return jax.shard_map(body, mesh=mesh, in_specs=in_specs, out_specs=out_specs, check_vma=False)
```

```python
import functools
import math

import jax
import jax.numpy as jnp
from jax import lax
from jax.experimental import pallas as pl
from jax.experimental.pallas import tpu as pltpu
from jax.sharding import PartitionSpec as P

TILE = 128
KW = 4096
NB_MOST = 8
DEGREE = 3
PAIR_MOST = 32
GROUP = 4

SIDE_CROSS = 8.0
NEAR_SQUARE = 0.36
NEAR_AMP = 0.15
FAR_AMP = 8.0
SPLIT_SQUARE = 64.0
SCREEN = 4.0
SAFETY = 1.25
SPREAD = 100.0
EPSILON = 1e-06

F32 = jnp.float32
BF16 = jnp.bfloat16
VMEM_LIMIT = 8 << 20

SINE = (4.44287968, -7.30781651, 3.59777427, -0.791199386)
ROUNDER = 12582912.0
COSINE = (1.4142040014266968, -6.97763729095459, 5.715188026428223, -1.728213906288147)


def split(x):
    high = x.astype(BF16)
    return high, (x - high.astype(F32)).astype(BF16)


def poly(coeffs, x):
    acc = coeffs[-1]
    for c in coeffs[-2::-1]:
        acc = acc * x + c
    return acc


def emit(kinds, terms, at, msg_ref):
    width = kinds[0].shape[1]
    t = terms[:, at : at + width]
    pieces = []
    for full in kinds:
        fx, fy, fz = full[0:8], full[8:16], full[16:24]
        pieces.append(t[1:2] * fx + t[2:3] * fy)
        pieces.append(t[3:4] * fx + t[4:5] * fy + t[5:6] * fz)
    stacked = jnp.concatenate(pieces, axis=0)
    for k in range(width // TILE):
        row = (at // TILE + k) * 32
        msg_ref[row : row + 32, :] = stacked[:, k * TILE : (k + 1) * TILE]


def product(both, high_table, low_table):
    first = jnp.dot(both, high_table, preferred_element_type=F32)
    second = jnp.dot(both[:24], low_table, preferred_element_type=F32)
    return first[:24] + (first[24:] + second)


def forward(rows, table_ref, terms, msg_ref):
    waves = table_ref.shape[2]
    both = jnp.concatenate(split(rows), axis=0)
    step = min(512, waves)
    for at in range(0, waves, step):
        cols = slice(at, at + step)
        kinds = [product(both, table_ref[k, :, cols], table_ref[2 + k, :, cols]) for k in range(2)]
        emit(kinds, terms, at, msg_ref)


def own_tiles(rows, share, rank, ranks):
    picked = []
    for k in range(share):
        tiles = [rows[:, t * TILE : (t + 1) * TILE] for t in range(k * ranks, (k + 1) * ranks)]
        mine = tiles[0]
        for r in range(1, ranks):
            mine = jnp.where(jnp.abs(rank - r) < 0.5, tiles[r], mine)
        picked.append(mine)
    return jnp.concatenate(picked, axis=0)


def start_kernel(
    length_x, share, stack_ref, table_ref, flip_ref, terms_ref, msg_ref, mask_ref, turn_ref, left_ref, sum_ref
):
    particles = table_ref.shape[1]
    waves = table_ref.shape[2]
    tiles = particles // TILE
    ranks = tiles // share
    sides = (length_x, SIDE_CROSS, SIDE_CROSS)
    counts = [stack_ref[27 + a : 28 + a, :waves] for a in range(3)]
    k1, k2, k3 = [2.0 * math.pi * counts[a] / sides[a] for a in range(3)]
    square = k1 * k1 + k2 * k2 + k3 * k3
    scaled = square / SPLIT_SQUARE
    weight = FAR_AMP * (1.0 + scaled) * jnp.exp(-scaled) / (KW * (square + SCREEN))
    flat_square = k1 * k1 + k2 * k2
    flat = 1.0 / jnp.sqrt(flat_square)
    both = 1.0 / jnp.sqrt(square * flat_square)
    terms_ref[...] = jnp.concatenate(
        [
            weight,
            -k2 * flat,
            k1 * flat,
            -k1 * k3 * both,
            -k2 * k3 * both,
            flat_square * both,
            stack_ref[30:32, :waves],
        ],
        axis=0,
    )
    mask_ref[...] = jnp.broadcast_to(stack_ref[30:31, :TILE], mask_ref.shape)
    noise = stack_ref[0:24, :particles]
    places = jnp.concatenate([stack_ref[24:27, :particles], jnp.zeros((5, particles), F32)], axis=0)
    base = waves // TILE * 32
    rank = stack_ref[31:32, :TILE]
    row = base + 8 + 24 * share
    msg_ref[base : base + 8, :] = jnp.zeros((8, TILE), F32)
    msg_ref[base + 8 : row, :] = own_tiles(noise, share, rank, ranks)
    msg_ref[row : row + 8 * share, :] = own_tiles(places, share, rank, ranks)
    left_ref[...] = jnp.concatenate(split(noise), axis=0)
    parts = []
    rest = jnp.concatenate([places[a : a + 1] / sides[a] for a in range(3)], axis=0)
    for _ in range(3):
        parts.append(rest.astype(BF16).astype(F32))
        rest = rest - parts[-1]
    turn_ref[...] = jnp.concatenate(parts + [jnp.zeros((7, particles), F32)], axis=0).T.astype(BF16)
    numbers = jnp.concatenate(counts * 3 + [jnp.zeros((7, waves), F32)], axis=0).astype(BF16)
    block = min(512, particles)
    wide = 256

    def make(rows):
        for at in range(0, waves, wide):
            turns = jnp.dot(turn_ref[rows, :], numbers[:, at : at + wide], preferred_element_type=F32)
            for j in range(0, wide, TILE):
                cols = slice(at + j, at + j + TILE)
                t = turns[:, j : j + TILE]
                r = t - ((t + ROUNDER) - ROUNDER)
                x = r * r
                s = r * poly(SINE, x)
                c = poly(COSINE, x)
                table_ref[0, rows, cols], table_ref[2, rows, cols] = split(1.0 - s * s)
                table_ref[1, rows, cols], table_ref[3, rows, cols] = split(s * c)

    def use(rows, first):
        for kind in range(2):
            for at in range(0, waves, wide):
                cols = slice(at, at + wide)
                piece = product(left_ref[:, rows], table_ref[kind, rows, cols], table_ref[2 + kind, rows, cols])
                sum_ref[kind, :, cols] = piece if first else sum_ref[kind, :, cols] + piece
        for kind in range(4):
            flip_ref[kind, :, rows] = table_ref[kind, rows, :].T

    blocks = [slice(at, at + block) for at in range(0, particles, block)]
    make(blocks[0])
    for k in range(1, len(blocks)):
        use(blocks[k - 1], k == 1)
        make(blocks[k])
    use(blocks[-1], len(blocks) == 1)
    emit([sum_ref[0], sum_ref[1]], terms_ref[...], 0, msg_ref)


def pair_kernel(length_x, base, share, meta_ref, lists_ref, counts_ref, pos_ref, own_ref, near_ref, away_ref, out_ref, plan_ref, place_ref, column_ref):
    tiles = lists_ref.shape[0]
    ranks = tiles // share
    odd = meta_ref[0] == 1
    rank = meta_ref[1]
    seen = jnp.int32(0)
    for target in range(tiles):
        for k in range(NB_MOST):
            window = lists_ref[target, k]
            side, tile = lax.div(window, tiles), lax.rem(window, tiles)
            which = jnp.where(side == 1, 0, jnp.where((side == 0) == odd, 1, 2))
            mine = (k < counts_ref[target]) & (lax.rem(tile, ranks) == rank)
            plan_ref[0, seen] = target
            plan_ref[1, seen] = which * share + lax.div(tile, ranks)
            plan_ref[2, seen] = jnp.where(window == tiles + target, 1, 0)
            seen = jnp.minimum(seen + jnp.where(mine, 1, 0), PAIR_MOST)
    plan_ref[3, 0] = seen
    for k in range(GROUP):
        plan_ref[0, seen + k] = tiles
        plan_ref[1, seen + k] = 0
    sides = (length_x, SIDE_CROSS, SIDE_CROSS)
    reach = math.sqrt(NEAR_SQUARE)
    filler = jnp.zeros((5, TILE), F32)
    for i in range(tiles):
        lanes = slice(i * TILE, (i + 1) * TILE)
        place_ref[i] = jnp.concatenate([pos_ref[a : a + 1, lanes] / sides[a] for a in range(3)] + [filler], axis=0)
    for slab, ref in enumerate((own_ref, near_ref, away_ref)):
        for i in range(share):
            row = (base if slab < 2 else 24 * share) + 8 * i
            place = ref[row : row + 8, :]
            place = jnp.concatenate([place[a : a + 1] / sides[a] for a in range(3)] + [filler], axis=0)
            column_ref[slab * share + i] = place.T
    count = 32

    def pair(p, carry):
        target = place_ref[plan_ref[0, p]]
        source = column_ref[plan_ref[1, p]]
        own = plan_ref[2, p].astype(F32)
        lines = [target[a : a + 1] for a in range(3)]
        for at in range(0, TILE, count):
            rows = slice(at, at + count)
            q = []
            for a in range(3):
                offset = lines[a] - jnp.broadcast_to(source[rows, a : a + 1], (count, TILE))
                offset = offset - jnp.floor(offset + 0.5)
                q.append(offset * (sides[a] / reach))
            square = q[0] * q[0] + q[1] * q[1] + q[2] * q[2]
            same = (
                lax.broadcasted_iota(jnp.int32, (count, TILE), 0) + at
                == lax.broadcasted_iota(jnp.int32, (count, TILE), 1)
            )
            envelope = jnp.exp(-square) * jnp.where(same, NEAR_AMP * (1.0 - own), NEAR_AMP)
            slot = 0
            for a in range(3):
                scaled = envelope * q[a]
                for b in range(a, 3):
                    value = scaled * q[b]
                    if a == b:
                        value = value + envelope
                    cols = slice(slot * TILE, (slot + 1) * TILE)
                    out_ref[p, rows, cols], out_ref[p, TILE + at : TILE + at + count, cols] = split(value)
                    slot += 1
        return carry

    lax.fori_loop(0, seen, pair, 0)


def near_kernel(base, share, plan_ref, own_ref, near_ref, away_ref, matrix_ref, out_ref, window_ref, sum_ref):
    tiles = sum_ref.shape[0] - 1
    for slab, ref in enumerate((own_ref, near_ref, away_ref)):
        for i in range(share):
            row = (base if slab < 2 else 0) + 24 * i
            window_ref[slab * share + i] = ref[row : row + 24, :]
    sum_ref[...] = jnp.zeros_like(sum_ref)

    def part(rows, at):
        return rows[:, at * TILE : (at + 1) * TILE]

    def several(at, carry):
        for k in range(GROUP):
            p = at * GROUP + k
            high, low = split(window_ref[plan_ref[1, p]])
            left = jnp.concatenate(
                [
                    jnp.concatenate([high, high], axis=1),
                    jnp.concatenate([low, jnp.zeros_like(low)], axis=1),
                ],
                axis=0,
            )
            both = jnp.dot(left, matrix_ref[p], preferred_element_type=F32)
            full = both[:24] + both[24:]
            x, y, z = full[0:8], full[8:16], full[16:24]
            sum_ref[plan_ref[0, p]] += jnp.concatenate(
                [
                    part(x, 0) + part(y, 1) + part(z, 2),
                    part(x, 1) + part(y, 3) + part(z, 4),
                    part(x, 2) + part(y, 4) + part(z, 5),
                ],
                axis=0,
            )
        return carry

    lax.fori_loop(0, lax.div(plan_ref[3, 0] + (GROUP - 1), GROUP), several, 0)
    for i in range(tiles):
        out_ref[:, i * TILE : (i + 1) * TILE] = sum_ref[i]


def back_kernel(parts, *refs):
    ins, (near_ref, terms_ref, flip_ref, out_ref, norm_ref, left_ref) = (
        refs[:parts],
        refs[parts:],
    )
    waves = terms_ref.shape[1]
    particles = out_ref.shape[1]
    tiles = waves // TILE
    norm = ins[0][32 * tiles : 32 * tiles + 8, :]
    for ref in ins[1:]:
        norm = norm + ref[32 * tiles : 32 * tiles + 8, :]
    norm_ref[...] = norm
    for i in range(tiles):
        block = ins[0][32 * i : 32 * i + 32, :]
        for ref in ins[1:]:
            block = block + ref[32 * i : 32 * i + 32, :]
        t = terms_ref[:, i * TILE : (i + 1) * TILE]
        block = block * t[0:1]
        for kind in range(2):
            one, two = block[16 * kind : 16 * kind + 8], block[16 * kind + 8 : 16 * kind + 16]
            rows = jnp.concatenate(
                [t[1:2] * one + t[3:4] * two, t[2:3] * one + t[4:5] * two, t[5:6] * two], axis=0
            )
            left_ref[kind, :, i * TILE : (i + 1) * TILE] = jnp.concatenate(split(rows), axis=0)
    step = min(512, particles)
    for at in range(0, particles, step):
        cols = slice(at, at + step)
        total = near_ref[:, cols]
        for k in range(2):
            total = total + product(left_ref[k], flip_ref[k, :, cols], flip_ref[2 + k, :, cols])
        out_ref[:, cols] = total


def step_kernel(parts, share, *refs):
    ins, (force_ref, terms_ref, table_ref, rows_ref, msg_ref) = refs[:parts], refs[parts:]
    particles = force_ref.shape[1]
    waves = terms_ref.shape[1]
    total = ins[0][...]
    for ref in ins[1:]:
        total = total + ref[...]
    rows = force_ref[...] + total
    rows_ref[...] = rows
    squares = rows * rows
    squares = squares[0:8] + squares[8:16] + squares[16:24]
    tiles = particles // TILE
    norm = squares[:, 0:TILE]
    for i in range(1, tiles):
        norm = norm + squares[:, i * TILE : (i + 1) * TILE]
    base = waves // TILE * 32
    msg_ref[base : base + 8, :] = norm
    msg_ref[base + 8 : base + 8 + 24 * share, :] = own_tiles(rows, share, terms_ref[7:8, :TILE], tiles // share)
    forward(rows, table_ref, terms_ref[...], msg_ref)


def final_kernel(parts, *refs):
    ins, (noise_ref, one_ref, two_ref, first_ref, second_ref, out_ref) = refs[:parts], refs[parts:]
    total = ins[0][...]
    for ref in ins[1:]:
        total = total + ref[...]
    u0, u1, u2 = noise_ref[...], one_ref[...], two_ref[...]
    u3 = u2 + total
    first = jnp.sum(first_ref[...], axis=1, keepdims=True)
    second = jnp.sum(second_ref[...], axis=1, keepdims=True)
    ratio = jnp.max(second / (first + EPSILON), axis=0, keepdims=True)
    high = SAFETY * jnp.sqrt(ratio)
    low = high / SPREAD
    nodes = DEGREE + 1
    angles = [math.pi * (j + 0.5) / nodes for j in range(nodes)]
    samples = [jnp.sqrt(0.5 * (high - low) * math.cos(t) + 0.5 * (high + low)) for t in angles]
    coeffs = []
    for k in range(nodes):
        acc = samples[0] * math.cos(k * angles[0])
        for j in range(1, nodes):
            acc = acc + samples[j] * math.cos(k * angles[j])
        coeffs.append(acc * (2.0 / nodes) * (0.5 if k == 0 else 1.0))
    p = 2.0 / (high - low)
    q = (high + low) / (high - low)
    v0, v1, v2 = p * u1 - q * u0, p * u2 - q * u1, p * u3 - q * u2
    t2 = 2.0 * (p * v1 - q * v0) - u0
    m2 = 2.0 * (p * v2 - q * v1) - u1
    t3 = 2.0 * (p * m2 - q * t2) - v0
    out_ref[...] = coeffs[0] * u0 + coeffs[1] * v0 + coeffs[2] * t2 + coeffs[3] * t3


def call(kernel, outs, args, scratch=(), smem_in=0, smem_out=(), flops=0, space=pltpu.VMEM):
    vmem = pl.BlockSpec(memory_space=pltpu.VMEM)
    smem = pl.BlockSpec(memory_space=pltpu.SMEM)
    return pl.pallas_call(
        kernel,
        out_shape=[jax.ShapeDtypeStruct(*o) for o in outs],
        in_specs=[smem] * smem_in + [pl.BlockSpec(memory_space=space)] * (len(args) - smem_in),
        out_specs=[smem if i in smem_out else vmem for i in range(len(outs))],
        scratch_shapes=list(scratch),
        cost_estimate=pl.CostEstimate(flops=flops, bytes_accessed=0, transcendentals=0),
        compiler_params=pltpu.CompilerParams(vmem_limit_bytes=VMEM_LIMIT),
    )(*args)


def exchange(x, axis, lowest):
    size = lax.axis_size(axis)
    bit = lowest
    parts = [x]
    while bit < size:
        if len(parts) > 1:
            x = functools.reduce(jnp.add, parts)
        radix = min(4, size // bit)
        parts = [x] + [
            lax.ppermute(x, axis, [(i, i ^ (d * bit)) for i in range(size)]) for d in range(1, radix)
        ]
        bit *= radix
    return parts


def chip_sums(chip, mask, away, work):
    size = lax.axis_size("space")
    done = None if work is None else work(away)
    if size != 8:
        return exchange(chip, "space", 2), away, done
    half = chip.shape[0] // 2
    low = mask < 0.5
    one = lax.ppermute(chip, "space", [(i, i ^ (4 if i % 2 else 2)) for i in range(size)])
    mine = jnp.where(low, chip[:half], chip[half:])
    across = lax.ppermute(mine, "space", [(i, i ^ 6) for i in range(size)])
    across, away, done = lax.optimization_barrier((across, away, done))
    both = jnp.concatenate([jnp.where(low, across, 0.0), jnp.where(low, 0.0, across)], axis=0)
    fetched = one + both
    return [chip, fetched, lax.ppermute(fetched, "space", [(i, i ^ 1) for i in range(size)])], away, done


def body(noise, positions, wave_index, tile_lists, tile_counts):
    slabs = lax.axis_size("space")
    length_x = float(slabs)
    vectors = noise.shape[0]
    particles = positions.shape[1]
    waves = wave_index.shape[1]
    tiles = particles // TILE
    ranks = lax.axis_size("wave")
    share = tiles // ranks
    place = jnp.stack([lax.axis_index("space") & 1, lax.axis_index("wave")]).astype(jnp.int32)
    core = [(i, i ^ 1) for i in range(slabs)]
    third = [(i, (i + 1 if i % 2 else i - 1) % slabs) for i in range(slabs)]
    table = ((4, particles, waves), BF16)
    rows_shape = ((3 * vectors, particles), F32)
    base = waves // TILE * 32 + 8
    far_flops = 2 * 96 * particles * waves * 2

    rows = jnp.transpose(noise, (1, 0, 2)).reshape(3 * vectors, particles)
    width = max(particles, waves)
    stack = jnp.concatenate(
        [
            jnp.pad(x.astype(F32), ((0, 0), (0, width - x.shape[1])))
            for x in (rows, positions, wave_index, jnp.broadcast_to(place[:, None], (2, width)))
        ],
        axis=0,
    )
    phases, flipped, terms, msg, mask = call(
        functools.partial(start_kernel, length_x, share),
        [
            table,
            ((4, waves, particles), BF16),
            ((8, waves), F32),
            ((base + 32 * share, TILE), F32),
            ((base // 2, TILE), F32),
        ],
        (stack,),
        [
            pltpu.VMEM((particles, 16), BF16),
            pltpu.VMEM((6 * vectors, particles), BF16),
            pltpu.VMEM((2, 3 * vectors, waves), F32),
        ],
        flops=4 * far_flops,
    )
    noise_rows = rows
    images, norms = [], []

    matrices = plan = None
    for step in range(DEGREE):
        other = lax.ppermute(msg, "space", core)
        away = lax.ppermute(msg[base:], "space", third)

        def pair_work(away):
            return call(
                functools.partial(pair_kernel, length_x, base + 24 * share, share),
                [((PAIR_MOST + GROUP, 2 * TILE, 6 * TILE), BF16), ((4, PAIR_MOST + GROUP), jnp.int32)],
                (place, tile_lists, tile_counts, positions, msg, other, away),
                [pltpu.VMEM((tiles, 8, TILE), F32), pltpu.VMEM((3 * share, TILE, 8), F32)],
                smem_in=3,
                smem_out=(1,),
                flops=far_flops,
            )

        def near_work():
            return call(
                functools.partial(near_kernel, base, share),
                [rows_shape],
                (plan, msg, other, away, matrices),
                [pltpu.VMEM((3 * share, 24, TILE), F32), pltpu.VMEM((tiles + 1, 24, TILE), F32)],
                smem_in=1,
                flops=far_flops // 2,
            )[0]

        factors, away, made = chip_sums(msg[:base] + other[:base], mask, away, pair_work if step == 0 else None)
        if step == 0:
            matrices, plan = made
        near_part = near_work()
        part, norm = call(
            functools.partial(back_kernel, len(factors)),
            [rows_shape, ((8, TILE), F32)],
            (*factors, near_part, terms, flipped),
            [pltpu.VMEM((2, 48, waves), BF16)],
            flops=far_flops,
        )
        norms.append(norm)
        sums = exchange(part, "wave", 1)
        if step < DEGREE - 1:
            rows, msg = call(
                functools.partial(step_kernel, len(sums), share),
                [rows_shape, ((base + 24 * share, TILE), F32)],
                (*sums, rows, terms, phases),
                flops=far_flops,
            )
            images.append(rows)
    out = call(
        functools.partial(final_kernel, len(sums)),
        [rows_shape],
        (*sums, noise_rows, *images, norms[1], norms[2]),
    )[0]
    return jnp.transpose(out.reshape(3, vectors, particles), (1, 0, 2))


def solution(mesh):
    in_specs = (
        P(None, None, "space"),
        P(None, "space"),
        P(None, "wave"),
        P("space", None),
        P("space"),
    )
    out_specs = P(None, None, "space")
    return jax.shard_map(body, mesh=mesh, in_specs=in_specs, out_specs=out_specs, check_vma=False)
```

```python
import functools
import math

import jax
import jax.numpy as jnp
from jax import lax
from jax.experimental import pallas as pl
from jax.experimental.pallas import tpu as pltpu
from jax.sharding import PartitionSpec as P

TILE = 128
KW = 4096
NB_MOST = 8
DEGREE = 3
PAIR_MOST = 32
GROUP = 4
SLOTS = PAIR_MOST + 2 * GROUP

SIDE_CROSS = 8.0
NEAR_SQUARE = 0.36
NEAR_AMP = 0.15
FAR_AMP = 8.0
SPLIT_SQUARE = 64.0
SCREEN = 4.0
SAFETY = 1.25
SPREAD = 100.0
EPSILON = 1e-06

F32 = jnp.float32
BF16 = jnp.bfloat16
VMEM_LIMIT = 8 << 20

SINE = (4.44287968, -7.30781651, 3.59777427, -0.791199386)
ROUNDER = 12582912.0
COSINE = (1.4142040014266968, -6.97763729095459, 5.715188026428223, -1.728213906288147)


def split(x):
    high = x.astype(BF16)
    return high, (x - high.astype(F32)).astype(BF16)


def poly(coeffs, x):
    acc = coeffs[-1]
    for c in coeffs[-2::-1]:
        acc = acc * x + c
    return acc


def emit(kinds, terms, at, msg_ref):
    width = kinds[0].shape[1]
    t = terms[:, at : at + width]
    pieces = []
    for full in kinds:
        fx, fy, fz = full[0:8], full[8:16], full[16:24]
        pieces.append(t[1:2] * fx + t[2:3] * fy)
        pieces.append(t[3:4] * fx + t[4:5] * fy + t[5:6] * fz)
    stacked = jnp.concatenate(pieces, axis=0)
    for k in range(width // TILE):
        row = (at // TILE + k) * 32
        msg_ref[row : row + 32, :] = stacked[:, k * TILE : (k + 1) * TILE]


def product(both, high_table, low_table):
    first = jnp.dot(both, high_table, preferred_element_type=F32)
    second = jnp.dot(both[:24], low_table, preferred_element_type=F32)
    return first[:24] + (first[24:] + second)


def forward(rows, table_ref, terms, msg_ref):
    waves = table_ref.shape[2]
    both = jnp.concatenate(split(rows), axis=0)
    step = min(512, waves)
    for at in range(0, waves, step):
        cols = slice(at, at + step)
        kinds = [product(both, table_ref[k, :, cols], table_ref[2 + k, :, cols]) for k in range(2)]
        emit(kinds, terms, at, msg_ref)


def own_tiles(rows, share, rank, ranks):
    picked = []
    for k in range(share):
        tiles = [rows[:, t * TILE : (t + 1) * TILE] for t in range(k * ranks, (k + 1) * ranks)]
        mine = tiles[0]
        for r in range(1, ranks):
            mine = jnp.where(jnp.abs(rank - r) < 0.5, tiles[r], mine)
        picked.append(mine)
    return jnp.concatenate(picked, axis=0)


def start_kernel(
    length_x, share, index_ref, place_ref, stack_ref, table_ref, flip_ref, terms_ref, msg_ref, mask_ref, turn_ref, left_ref, sum_ref
):
    particles = table_ref.shape[1]
    waves = table_ref.shape[2]
    tiles = particles // TILE
    ranks = tiles // share
    sides = (length_x, SIDE_CROSS, SIDE_CROSS)
    counts = [index_ref[a : a + 1, :].astype(F32) for a in range(3)]
    core = place_ref[0:1]
    rank = place_ref[1:2]
    k1, k2, k3 = [2.0 * math.pi * counts[a] / sides[a] for a in range(3)]
    square = k1 * k1 + k2 * k2 + k3 * k3
    scaled = square / SPLIT_SQUARE
    weight = FAR_AMP * (1.0 + scaled) * jnp.exp(-scaled) / (KW * (square + SCREEN))
    flat_square = k1 * k1 + k2 * k2
    flat = 1.0 / jnp.sqrt(flat_square)
    both = 1.0 / jnp.sqrt(square * flat_square)
    terms_ref[...] = jnp.concatenate(
        [
            weight,
            -k2 * flat,
            k1 * flat,
            -k1 * k3 * both,
            -k2 * k3 * both,
            flat_square * both,
            jnp.concatenate([place_ref[...]] * (waves // TILE), axis=1),
        ],
        axis=0,
    )
    mask_ref[...] = jnp.broadcast_to(core, mask_ref.shape)
    noise = stack_ref[0:24, :particles]
    places = jnp.concatenate([stack_ref[24:27, :particles], jnp.zeros((5, particles), F32)], axis=0)
    base = waves // TILE * 32
    row = base + 8 + 24 * share
    msg_ref[base : base + 8, :] = jnp.zeros((8, TILE), F32)
    msg_ref[base + 8 : row, :] = own_tiles(noise, share, rank, ranks)
    msg_ref[row : row + 8 * share, :] = own_tiles(places, share, rank, ranks)
    left_ref[...] = jnp.concatenate(split(noise), axis=0)
    parts = []
    rest = jnp.concatenate([places[a : a + 1] / sides[a] for a in range(3)], axis=0)
    for _ in range(3):
        parts.append(rest.astype(BF16).astype(F32))
        rest = rest - parts[-1]
    turn_ref[...] = jnp.concatenate(parts + [jnp.zeros((7, particles), F32)], axis=0).T.astype(BF16)
    numbers = jnp.concatenate(counts * 3 + [jnp.zeros((7, waves), F32)], axis=0).astype(BF16)
    wide = 256

    def make(rows):
        for at in range(0, waves, wide):
            turns = jnp.dot(turn_ref[rows, :], numbers[:, at : at + wide], preferred_element_type=F32)
            for j in range(0, wide, TILE):
                cols = slice(at + j, at + j + TILE)
                t = turns[:, j : j + TILE]
                r = t - ((t + ROUNDER) - ROUNDER)
                x = r * r
                s = r * poly(SINE, x)
                c = poly(COSINE, x)
                table_ref[0, rows, cols], table_ref[2, rows, cols] = split(1.0 - s * s)
                table_ref[1, rows, cols], table_ref[3, rows, cols] = split(s * c)

    def use(rows, first):
        for kind in range(2):
            for at in range(0, waves, wide):
                cols = slice(at, at + wide)
                piece = product(left_ref[:, rows], table_ref[kind, rows, cols], table_ref[2 + kind, rows, cols])
                sum_ref[kind, :, cols] = piece if first else sum_ref[kind, :, cols] + piece
        for kind in range(4):
            flip_ref[kind, :, rows] = table_ref[kind, rows, :].T

    ends = [0] + [particles * k // 8 for k in (4, 6, 8)]
    blocks = [slice(low, high) for low, high in zip(ends, ends[1:])]
    make(blocks[0])
    for k in range(1, len(blocks)):
        use(blocks[k - 1], k == 1)
        make(blocks[k])
    use(blocks[-1], len(blocks) == 1)
    emit([sum_ref[0], sum_ref[1]], terms_ref[...], 0, msg_ref)


def pair_kernel(length_x, base, share, core_ref, live_ref, pos_ref, own_ref, near_ref, away_ref, out_ref, plan_ref, place_ref, column_ref):
    tiles = pos_ref.shape[1] // TILE
    ranks = tiles // share
    odd = core_ref[0] == 1
    rank = core_ref[1]
    inner = outer = jnp.int32(0)
    for target in range(tiles):
        for k in range(NB_MOST):
            window = live_ref[target, k]
            side, tile = lax.div(window, tiles), lax.rem(window, tiles)
            which = jnp.where(side == 1, 0, jnp.where((side == 0) == odd, 1, 2))
            mine = jnp.where((window >= 0) & (lax.rem(tile, ranks) == rank), 1, 0)
            third = jnp.where(which == 2, 1, 0)
            at = jnp.where(which == 2, SLOTS - 1 - outer, inner)
            plan_ref[0, at] = target
            plan_ref[1, at] = which * share + lax.div(tile, ranks)
            plan_ref[2, at] = jnp.where(window == tiles + target, 1, 0)
            inner = jnp.minimum(inner + mine * (1 - third), PAIR_MOST)
            outer = jnp.minimum(outer + mine * third, PAIR_MOST)
    plan_ref[3, 0] = inner
    plan_ref[3, 1] = outer
    for k in range(GROUP):
        for at in (inner + k, SLOTS - 1 - outer - k):
            plan_ref[0, at] = tiles
            plan_ref[1, at] = 0
    sides = (length_x, SIDE_CROSS, SIDE_CROSS)
    reach = math.sqrt(NEAR_SQUARE)
    filler = jnp.zeros((5, TILE), F32)
    for i in range(tiles):
        lanes = slice(i * TILE, (i + 1) * TILE)
        place_ref[i] = jnp.concatenate([pos_ref[24 + a : 25 + a, lanes] / sides[a] for a in range(3)] + [filler], axis=0)
    for slab, ref in enumerate((own_ref, near_ref, away_ref)):
        for i in range(share):
            row = (base if slab < 2 else 24 * share) + 8 * i
            place = ref[row : row + 8, :]
            place = jnp.concatenate([place[a : a + 1] / sides[a] for a in range(3)] + [filler], axis=0)
            column_ref[slab * share + i] = place.T
    count = 32

    def pair(at, carry):
        p = jnp.where(at < inner, at, SLOTS - 1 + inner - at)
        target = place_ref[plan_ref[0, p]]
        source = column_ref[plan_ref[1, p]]
        own = plan_ref[2, p].astype(F32)
        lines = [target[a : a + 1] for a in range(3)]
        for low in range(0, TILE, count):
            rows = slice(low, low + count)
            q = []
            for a in range(3):
                offset = lines[a] - jnp.broadcast_to(source[rows, a : a + 1], (count, TILE))
                offset = offset - jnp.floor(offset + 0.5)
                q.append(offset * (sides[a] / reach))
            square = q[0] * q[0] + q[1] * q[1] + q[2] * q[2]
            same = (
                lax.broadcasted_iota(jnp.int32, (count, TILE), 0) + low
                == lax.broadcasted_iota(jnp.int32, (count, TILE), 1)
            )
            envelope = jnp.exp(-square) * jnp.where(same, NEAR_AMP * (1.0 - own), NEAR_AMP)
            slot = 0
            for a in range(3):
                scaled = envelope * q[a]
                for b in range(a, 3):
                    value = scaled * q[b]
                    if a == b:
                        value = value + envelope
                    cols = slice(slot * TILE, (slot + 1) * TILE)
                    out_ref[p, rows, cols], out_ref[p, TILE + low : TILE + low + count, cols] = split(value)
                    slot += 1
        return carry

    lax.fori_loop(0, inner + outer, pair, 0)


def near_kernel(base, share, within, beyond, plan_ref, *refs):
    matrix_ref, out_ref, window_ref, sum_ref = refs[-4:]
    sources = list(refs[:-4])
    before_ref = None if within else sources.pop()
    slabs = [(0, base), (1, base)] * within + [(2, 0)] * beyond
    slabs = [(slab, ref, start) for (slab, start), ref in zip(slabs, sources)]
    tiles = sum_ref.shape[0] - 1
    for slab, ref, start in slabs:
        for i in range(share):
            row = start + 24 * i
            window_ref[slab * share + i] = ref[row : row + 24, :]
    if before_ref is None:
        sum_ref[...] = jnp.zeros_like(sum_ref)
    else:
        for i in range(tiles):
            sum_ref[i] = before_ref[:, i * TILE : (i + 1) * TILE]
        sum_ref[tiles] = jnp.zeros_like(sum_ref[tiles])

    def part(rows, at):
        return rows[:, at * TILE : (at + 1) * TILE]

    def add(p):
        high, low = split(window_ref[plan_ref[1, p]])
        left = jnp.concatenate(
            [
                jnp.concatenate([high, high], axis=1),
                jnp.concatenate([low, jnp.zeros_like(low)], axis=1),
            ],
            axis=0,
        )
        both = jnp.dot(left, matrix_ref[p], preferred_element_type=F32)
        full = both[:24] + both[24:]
        x, y, z = full[0:8], full[8:16], full[16:24]
        sum_ref[plan_ref[0, p]] += jnp.concatenate(
            [
                part(x, 0) + part(y, 1) + part(z, 2),
                part(x, 1) + part(y, 3) + part(z, 4),
                part(x, 2) + part(y, 4) + part(z, 5),
            ],
            axis=0,
        )

    for wanted, row, start, step in ((within, 0, 0, 1), (beyond, 1, SLOTS - 1, -1)):
        if wanted:

            def several(at, carry):
                for k in range(GROUP):
                    add(start + step * (at * GROUP + k))
                return carry

            lax.fori_loop(0, lax.div(plan_ref[3, row] + (GROUP - 1), GROUP), several, 0)
    for i in range(tiles):
        out_ref[:, i * TILE : (i + 1) * TILE] = sum_ref[i]


def back_kernel(parts, *refs):
    ins, (near_ref, terms_ref, flip_ref, out_ref) = refs[:parts], refs[parts : parts + 4]
    norm_refs, left_ref = refs[parts + 4 : -1], refs[-1]
    waves = terms_ref.shape[1]
    particles = out_ref.shape[1]
    tiles = waves // TILE
    for norm_ref in norm_refs:
        norm = ins[0][32 * tiles : 32 * tiles + 8, :]
        for ref in ins[1:]:
            norm = norm + ref[32 * tiles : 32 * tiles + 8, :]
        norm_ref[...] = norm
    for i in range(tiles):
        block = ins[0][32 * i : 32 * i + 32, :]
        for ref in ins[1:]:
            block = block + ref[32 * i : 32 * i + 32, :]
        t = terms_ref[:, i * TILE : (i + 1) * TILE]
        block = block * t[0:1]
        for kind in range(2):
            one, two = block[16 * kind : 16 * kind + 8], block[16 * kind + 8 : 16 * kind + 16]
            rows = jnp.concatenate(
                [t[1:2] * one + t[3:4] * two, t[2:3] * one + t[4:5] * two, t[5:6] * two], axis=0
            )
            left_ref[kind, :, i * TILE : (i + 1) * TILE] = jnp.concatenate(split(rows), axis=0)
    step = min(512, particles)
    for at in range(0, particles, step):
        cols = slice(at, at + step)
        total = near_ref[:, cols]
        for k in range(2):
            total = total + product(left_ref[k], flip_ref[k, :, cols], flip_ref[2 + k, :, cols])
        out_ref[:, cols] = total


def next_kernel(parts, share, *refs):
    ins, (force_ref, terms_ref, rows_ref, tiles_ref, norm_ref) = refs[:parts], refs[parts:]
    particles = force_ref.shape[1]
    total = ins[0][...]
    for ref in ins[1:]:
        total = total + ref[...]
    rows = force_ref[...] + total
    rows_ref[...] = rows
    tiles_ref[...] = own_tiles(rows, share, terms_ref[7:8, :TILE], particles // TILE // share)
    squares = rows * rows
    squares = squares[0:8] + squares[8:16] + squares[16:24]
    norm = squares[:, 0:TILE]
    for i in range(1, particles // TILE):
        norm = norm + squares[:, i * TILE : (i + 1) * TILE]
    norm_ref[...] = norm


def factor_kernel(rows_ref, tiles_ref, norm_ref, terms_ref, table_ref, msg_ref):
    base = terms_ref.shape[1] // TILE * 32
    msg_ref[base : base + 8, :] = norm_ref[...]
    msg_ref[base + 8 :, :] = tiles_ref[...]
    forward(rows_ref[...], table_ref, terms_ref[...], msg_ref)


def final_kernel(parts, *refs):
    ins, (noise_ref, one_ref, two_ref, first_ref, second_ref, out_ref) = refs[:parts], refs[parts:]
    total = ins[0][...]
    for ref in ins[1:]:
        total = total + ref[...]
    u0, u1, u2 = noise_ref[...], one_ref[...], two_ref[...]
    u3 = u2 + total
    first = jnp.sum(first_ref[...], axis=1, keepdims=True)
    second = jnp.sum(second_ref[...], axis=1, keepdims=True)
    ratio = jnp.max(second / (first + EPSILON), axis=0, keepdims=True)
    high = SAFETY * jnp.sqrt(ratio)
    low = high / SPREAD
    nodes = DEGREE + 1
    angles = [math.pi * (j + 0.5) / nodes for j in range(nodes)]
    samples = [jnp.sqrt(0.5 * (high - low) * math.cos(t) + 0.5 * (high + low)) for t in angles]
    coeffs = []
    for k in range(nodes):
        acc = samples[0] * math.cos(k * angles[0])
        for j in range(1, nodes):
            acc = acc + samples[j] * math.cos(k * angles[j])
        coeffs.append(acc * (2.0 / nodes) * (0.5 if k == 0 else 1.0))
    p = 2.0 / (high - low)
    q = (high + low) / (high - low)
    v0, v1, v2 = p * u1 - q * u0, p * u2 - q * u1, p * u3 - q * u2
    t2 = 2.0 * (p * v1 - q * v0) - u0
    m2 = 2.0 * (p * v2 - q * v1) - u1
    t3 = 2.0 * (p * m2 - q * t2) - v0
    out_ref[...] = coeffs[0] * u0 + coeffs[1] * v0 + coeffs[2] * t2 + coeffs[3] * t3


def call(kernel, outs, args, scratch=(), smem_in=0, smem_out=(), flops=0, space=pltpu.VMEM):
    vmem = pl.BlockSpec(memory_space=pltpu.VMEM)
    smem = pl.BlockSpec(memory_space=pltpu.SMEM)
    return pl.pallas_call(
        kernel,
        out_shape=[jax.ShapeDtypeStruct(*o) for o in outs],
        in_specs=[smem] * smem_in + [pl.BlockSpec(memory_space=space)] * (len(args) - smem_in),
        out_specs=[smem if i in smem_out else vmem for i in range(len(outs))],
        scratch_shapes=list(scratch),
        cost_estimate=pl.CostEstimate(flops=flops, bytes_accessed=0, transcendentals=0),
        compiler_params=pltpu.CompilerParams(vmem_limit_bytes=VMEM_LIMIT),
    )(*args)


def exchange(x, axis, lowest):
    size = lax.axis_size(axis)
    bit = lowest
    parts = [x]
    while bit < size:
        if len(parts) > 1:
            x = functools.reduce(jnp.add, parts)
        radix = min(4, size // bit)
        parts = [x] + [
            lax.ppermute(x, axis, [(i, i ^ (d * bit)) for i in range(size)]) for d in ((2, 1, 3) if radix == 4 else range(1, radix))
        ]
        bit *= radix
    return parts


def chip_sums(chip, mask, send_away, work):
    size = lax.axis_size("space")
    if size != 8:
        away = send_away()
        return exchange(chip, "space", 2), away, work(away)
    half = chip.shape[0] // 2
    low = mask < 0.5
    mine = jnp.where(low, chip[:half], chip[half:])
    away = send_away()
    one = lax.ppermute(chip, "space", [(i, i ^ (4 if i % 2 else 2)) for i in range(size)])
    across = lax.ppermute(mine, "space", [(i, i ^ 6) for i in range(size)])
    done = work(away)
    one, done = lax.optimization_barrier((one, done))
    across, away = lax.optimization_barrier((across, away))
    both = jnp.concatenate([jnp.where(low, across, 0.0), jnp.where(low, 0.0, across)], axis=0)
    fetched = one + both
    return [chip, fetched, lax.ppermute(fetched, "space", [(i, i ^ 1) for i in range(size)])], away, done


def body(noise, positions, wave_index, tile_lists, tile_counts):
    slabs = lax.axis_size("space")
    length_x = float(slabs)
    vectors = noise.shape[0]
    particles = positions.shape[1]
    waves = wave_index.shape[1]
    tiles = particles // TILE
    ranks = lax.axis_size("wave")
    share = tiles // ranks
    place = jnp.stack([lax.axis_index("space") & 1, lax.axis_index("wave")]).astype(jnp.int32)
    live = jnp.where(jnp.arange(NB_MOST)[None] < tile_counts[:, None], tile_lists, -1)
    core = [(i, i ^ 1) for i in range(slabs)]
    third = [(i, (i + 1 if i % 2 else i - 1) % slabs) for i in range(slabs)]
    table = ((4, particles, waves), BF16)
    rows_shape = ((3 * vectors, particles), F32)
    base = waves // TILE * 32 + 8
    far_flops = 2 * 96 * particles * waves * 2

    rows = jnp.transpose(noise, (1, 0, 2)).reshape(3 * vectors, particles)
    lines = jnp.broadcast_to(place.astype(F32)[:, None], (2, TILE))
    stack = jnp.concatenate([rows, positions], axis=0)
    phases, flipped, terms, msg, mask = call(
        functools.partial(start_kernel, length_x, share),
        [
            table,
            ((4, waves, particles), BF16),
            ((8, waves), F32),
            ((base + 32 * share, TILE), F32),
            ((base // 2, TILE), F32),
        ],
        (wave_index, lines, stack),
        [
            pltpu.VMEM((particles, 16), BF16),
            pltpu.VMEM((6 * vectors, particles), BF16),
            pltpu.VMEM((2, 3 * vectors, waves), F32),
        ],
        flops=4 * far_flops,
    )
    noise_rows = rows
    images, norms = [], []

    matrices = plan = None
    for step in range(DEGREE):
        other = lax.ppermute(msg, "space", core)
        def send_away():
            return lax.ppermute(msg[base:] if step == 0 else own, "space", third)


        def pair_work(away):
            return call(
                functools.partial(pair_kernel, length_x, base + 24 * share, share),
                [((SLOTS, 2 * TILE, 6 * TILE), BF16), ((4, SLOTS), jnp.int32)],
                (place, live, stack, msg, other, away),
                [pltpu.VMEM((tiles, 8, TILE), F32), pltpu.VMEM((3 * share, TILE, 8), F32)],
                smem_in=2,
                smem_out=(1,),
                flops=far_flops,
            )

        def near_work(within, beyond, *sources):
            return call(
                functools.partial(near_kernel, base, share, within, beyond),
                [rows_shape],
                (plan, *sources, matrices),
                [pltpu.VMEM((3 * share, 24, TILE), F32), pltpu.VMEM((tiles + 1, 24, TILE), F32)],
                smem_in=1,
                flops=far_flops // 2,
            )[0]

        if step == 0:
            other, live = lax.optimization_barrier((other, live))
        chip = msg[:base] + other[:base]
        if step == 0:
            factors, away, (matrices, plan) = chip_sums(chip, mask, send_away, pair_work)
            near_part = near_work(True, True, msg, other, away)
        else:
            factors, away, near_part = chip_sums(
                chip, mask, send_away, lambda away: near_work(True, False, msg, other)
            )
            near_part = near_work(False, True, away, near_part)
        part, *norm = call(
            functools.partial(back_kernel, len(factors)),
            [rows_shape] + [((8, TILE), F32)] * (step > 0),
            (*factors, near_part, terms, flipped),
            [pltpu.VMEM((2, 48, waves), BF16)],
            flops=far_flops,
        )
        norms += norm
        sums = exchange(part, "wave", 1)
        if step < DEGREE - 1:
            rows, own, norm = call(
                functools.partial(next_kernel, len(sums), share),
                [rows_shape, ((24 * share, TILE), F32), ((8, TILE), F32)],
                (*sums, rows, terms),
                flops=1,
            )
            msg = call(
                factor_kernel,
                [((base + 24 * share, TILE), F32)],
                (rows, own, norm, terms, phases),
                flops=far_flops,
            )[0]
            images.append(rows)
    out = call(
        functools.partial(final_kernel, len(sums)),
        [rows_shape],
        (*sums, noise_rows, *images, *norms),
    )[0]
    return jnp.transpose(out.reshape(3, vectors, particles), (1, 0, 2))


def solution(mesh):
    in_specs = (
        P(None, None, "space"),
        P(None, "space"),
        P(None, "wave"),
        P("space", None),
        P("space"),
    )
    out_specs = P(None, None, "space")
    return jax.shard_map(body, mesh=mesh, in_specs=in_specs, out_specs=out_specs, check_vma=False)
```

```python
import functools
import math

import jax
import jax.numpy as jnp
from jax import lax
from jax.experimental import pallas as pl
from jax.experimental.pallas import tpu as pltpu
from jax.sharding import PartitionSpec as P

TILE = 128
KW = 4096
NB_MOST = 8
DEGREE = 3
PAIR_MOST = 32
GROUP = 4
SLOTS = PAIR_MOST + 2 * GROUP

SIDE_CROSS = 8.0
NEAR_SQUARE = 0.36
NEAR_AMP = 0.15
FAR_AMP = 8.0
SPLIT_SQUARE = 64.0
SCREEN = 4.0
SAFETY = 1.25
SPREAD = 100.0
EPSILON = 1e-06

F32 = jnp.float32
BF16 = jnp.bfloat16
VMEM_LIMIT = 8 << 20

SINE = (4.44287968, -7.30781651, 3.59777427, -0.791199386)
ROUNDER = 12582912.0
COSINE = (1.4142040014266968, -6.97763729095459, 5.715188026428223, -1.728213906288147)


def split(x):
    high = x.astype(BF16)
    return high, (x - high.astype(F32)).astype(BF16)


def poly(coeffs, x):
    acc = coeffs[-1]
    for c in coeffs[-2::-1]:
        acc = acc * x + c
    return acc


def emit(kinds, terms, at, mine_ref, rest_ref):
    width = kinds[0].shape[1]
    t = terms[:, at : at + width]
    pieces = []
    for full in kinds:
        fx, fy, fz = full[0:8], full[8:16], full[16:24]
        pieces.append(t[1:2] * fx + t[2:3] * fy)
        pieces.append(t[3:4] * fx + t[4:5] * fy + t[5:6] * fz)
    stacked = jnp.concatenate(pieces, axis=0)
    half = mine_ref.shape[0]
    for k in range(width // TILE):
        row = (at // TILE + k) * 32
        ref, row = (mine_ref, row) if row < half else (rest_ref, row - half)
        ref[row : row + 32, :] = stacked[:, k * TILE : (k + 1) * TILE]


def product(both, high_table, low_table):
    first = jnp.dot(both, high_table, preferred_element_type=F32)
    second = jnp.dot(both[:24], low_table, preferred_element_type=F32)
    return first[:24] + (first[24:] + second)


def forward(rows, table_ref, terms, mine_ref, rest_ref):
    waves = table_ref.shape[2]
    both = jnp.concatenate(split(rows), axis=0)
    step = min(512, waves)
    for at in range(0, waves, step):
        cols = slice(at, at + step)
        kinds = [product(both, table_ref[k, :, cols], table_ref[2 + k, :, cols]) for k in range(2)]
        emit(kinds, terms, at, mine_ref, rest_ref)


def own_tiles(rows, share, rank, ranks):
    picked = []
    for k in range(share):
        tiles = [rows[:, t * TILE : (t + 1) * TILE] for t in range(k * ranks, (k + 1) * ranks)]
        mine = tiles[0]
        for r in range(1, ranks):
            mine = jnp.where(jnp.abs(rank - r) < 0.5, tiles[r], mine)
        picked.append(mine)
    return jnp.concatenate(picked, axis=0)


def start_kernel(
    length_x, share, index_ref, place_ref, stack_ref, table_ref, flip_ref, terms_ref, mine_ref, rest_ref,
    turn_ref, left_ref, sum_ref
):
    particles = table_ref.shape[1]
    waves = table_ref.shape[2]
    tiles = particles // TILE
    ranks = tiles // share
    sides = (length_x, SIDE_CROSS, SIDE_CROSS)
    core = place_ref[0:1]
    rank = place_ref[1:2]
    whole = index_ref[...].astype(F32)
    turned = jnp.concatenate([whole[:, waves // 2 :], whole[:, : waves // 2]], axis=1)
    first = jnp.broadcast_to(jnp.concatenate([core] * (waves // TILE), axis=1), whole.shape) < 0.5
    whole = jnp.where(first, whole, turned)
    counts = [whole[a : a + 1] for a in range(3)]
    k1, k2, k3 = [2.0 * math.pi * counts[a] / sides[a] for a in range(3)]
    square = k1 * k1 + k2 * k2 + k3 * k3
    scaled = square / SPLIT_SQUARE
    weight = FAR_AMP * (1.0 + scaled) * jnp.exp(-scaled) / (KW * (square + SCREEN))
    flat_square = k1 * k1 + k2 * k2
    flat = 1.0 / jnp.sqrt(flat_square)
    both = 1.0 / jnp.sqrt(square * flat_square)
    terms_ref[...] = jnp.concatenate(
        [
            weight,
            -k2 * flat,
            k1 * flat,
            -k1 * k3 * both,
            -k2 * k3 * both,
            flat_square * both,
            jnp.concatenate([place_ref[...]] * (waves // TILE), axis=1),
        ],
        axis=0,
    )
    noise = stack_ref[0:24, :particles]
    places = jnp.concatenate([stack_ref[24:27, :particles], jnp.zeros((5, particles), F32)], axis=0)
    base = waves // TILE * 16
    row = base + 8 + 24 * share
    rest_ref[base : base + 8, :] = jnp.zeros((8, TILE), F32)
    rest_ref[base + 8 : row, :] = own_tiles(noise, share, rank, ranks)
    rest_ref[row : row + 8 * share, :] = own_tiles(places, share, rank, ranks)
    left_ref[...] = jnp.concatenate(split(noise), axis=0)
    parts = []
    rest = jnp.concatenate([places[a : a + 1] / sides[a] for a in range(3)], axis=0)
    for _ in range(3):
        parts.append(rest.astype(BF16).astype(F32))
        rest = rest - parts[-1]
    turn_ref[...] = jnp.concatenate(parts + [jnp.zeros((7, particles), F32)], axis=0).T.astype(BF16)
    numbers = jnp.concatenate(counts * 3 + [jnp.zeros((7, waves), F32)], axis=0).astype(BF16)
    wide = 256

    def make(rows):
        for at in range(0, waves, wide):
            turns = jnp.dot(turn_ref[rows, :], numbers[:, at : at + wide], preferred_element_type=F32)
            for j in range(0, wide, TILE):
                cols = slice(at + j, at + j + TILE)
                t = turns[:, j : j + TILE]
                r = t - ((t + ROUNDER) - ROUNDER)
                x = r * r
                s = r * poly(SINE, x)
                c = poly(COSINE, x)
                table_ref[0, rows, cols], table_ref[2, rows, cols] = split(1.0 - s * s)
                table_ref[1, rows, cols], table_ref[3, rows, cols] = split(s * c)

    def use(rows, first):
        for kind in range(2):
            for at in range(0, waves, wide):
                cols = slice(at, at + wide)
                piece = product(left_ref[:, rows], table_ref[kind, rows, cols], table_ref[2 + kind, rows, cols])
                sum_ref[kind, :, cols] = piece if first else sum_ref[kind, :, cols] + piece
        for kind in range(4):
            flip_ref[kind, :, rows] = table_ref[kind, rows, :].T

    ends = [0] + [particles * k // 8 for k in (4, 6, 8)]
    blocks = [slice(low, high) for low, high in zip(ends, ends[1:])]
    make(blocks[0])
    for k in range(1, len(blocks)):
        use(blocks[k - 1], k == 1)
        make(blocks[k])
    use(blocks[-1], len(blocks) == 1)
    emit([sum_ref[0], sum_ref[1]], terms_ref[...], 0, mine_ref, rest_ref)


def pair_kernel(length_x, base, share, core_ref, live_ref, pos_ref, own_ref, near_ref, away_ref, out_ref, plan_ref, place_ref, column_ref):
    tiles = pos_ref.shape[1] // TILE
    ranks = tiles // share
    odd = core_ref[0] == 1
    rank = core_ref[1]
    inner = outer = jnp.int32(0)
    for target in range(tiles):
        for k in range(NB_MOST):
            window = live_ref[target, k]
            side, tile = lax.div(window, tiles), lax.rem(window, tiles)
            which = jnp.where(side == 1, 0, jnp.where((side == 0) == odd, 1, 2))
            mine = jnp.where((window >= 0) & (lax.rem(tile, ranks) == rank), 1, 0)
            third = jnp.where(which == 2, 1, 0)
            at = jnp.where(which == 2, SLOTS - 1 - outer, inner)
            plan_ref[0, at] = target
            plan_ref[1, at] = which * share + lax.div(tile, ranks)
            plan_ref[2, at] = jnp.where(window == tiles + target, 1, 0)
            inner = jnp.minimum(inner + mine * (1 - third), PAIR_MOST)
            outer = jnp.minimum(outer + mine * third, PAIR_MOST)
    plan_ref[3, 0] = inner
    plan_ref[3, 1] = outer
    for k in range(GROUP):
        for at in (inner + k, SLOTS - 1 - outer - k):
            plan_ref[0, at] = tiles
            plan_ref[1, at] = 0
    sides = (length_x, SIDE_CROSS, SIDE_CROSS)
    reach = math.sqrt(NEAR_SQUARE)
    filler = jnp.zeros((5, TILE), F32)
    for i in range(tiles):
        lanes = slice(i * TILE, (i + 1) * TILE)
        place_ref[i] = jnp.concatenate([pos_ref[24 + a : 25 + a, lanes] / sides[a] for a in range(3)] + [filler], axis=0)
    for slab, ref in enumerate((own_ref, near_ref, away_ref)):
        for i in range(share):
            row = (base if slab < 2 else 24 * share) + 8 * i
            place = ref[row : row + 8, :]
            place = jnp.concatenate([place[a : a + 1] / sides[a] for a in range(3)] + [filler], axis=0)
            column_ref[slab * share + i] = place.T
    count = 32

    def pair(at, carry):
        p = jnp.where(at < inner, at, SLOTS - 1 + inner - at)
        target = place_ref[plan_ref[0, p]]
        source = column_ref[plan_ref[1, p]]
        own = plan_ref[2, p].astype(F32)
        lines = [target[a : a + 1] for a in range(3)]
        for low in range(0, TILE, count):
            rows = slice(low, low + count)
            q = []
            for a in range(3):
                offset = lines[a] - jnp.broadcast_to(source[rows, a : a + 1], (count, TILE))
                offset = offset - jnp.floor(offset + 0.5)
                q.append(offset * (sides[a] / reach))
            square = q[0] * q[0] + q[1] * q[1] + q[2] * q[2]
            same = (
                lax.broadcasted_iota(jnp.int32, (count, TILE), 0) + low
                == lax.broadcasted_iota(jnp.int32, (count, TILE), 1)
            )
            envelope = jnp.exp(-square) * jnp.where(same, NEAR_AMP * (1.0 - own), NEAR_AMP)
            slot = 0
            for a in range(3):
                scaled = envelope * q[a]
                for b in range(a, 3):
                    value = scaled * q[b]
                    if a == b:
                        value = value + envelope
                    cols = slice(slot * TILE, (slot + 1) * TILE)
                    out_ref[p, rows, cols], out_ref[p, TILE + low : TILE + low + count, cols] = split(value)
                    slot += 1
        return carry

    lax.fori_loop(0, inner + outer, pair, 0)


def near_kernel(base, share, within, beyond, plan_ref, *refs):
    matrix_ref, out_ref, window_ref, sum_ref = refs[-4:]
    sources = list(refs[:-4])
    before_ref = None if within else sources.pop()
    slabs = [(0, base), (1, base)] * within + [(2, 0)] * beyond
    slabs = [(slab, ref, start) for (slab, start), ref in zip(slabs, sources)]
    tiles = sum_ref.shape[0] - 1
    for slab, ref, start in slabs:
        for i in range(share):
            row = start + 24 * i
            window_ref[slab * share + i] = ref[row : row + 24, :]
    if before_ref is None:
        sum_ref[...] = jnp.zeros_like(sum_ref)
    else:
        for i in range(tiles):
            sum_ref[i] = before_ref[:, i * TILE : (i + 1) * TILE]
        sum_ref[tiles] = jnp.zeros_like(sum_ref[tiles])

    def part(rows, at):
        return rows[:, at * TILE : (at + 1) * TILE]

    def add(p):
        high, low = split(window_ref[plan_ref[1, p]])
        left = jnp.concatenate(
            [
                jnp.concatenate([high, high], axis=1),
                jnp.concatenate([low, jnp.zeros_like(low)], axis=1),
            ],
            axis=0,
        )
        both = jnp.dot(left, matrix_ref[p], preferred_element_type=F32)
        full = both[:24] + both[24:]
        x, y, z = full[0:8], full[8:16], full[16:24]
        sum_ref[plan_ref[0, p]] += jnp.concatenate(
            [
                part(x, 0) + part(y, 1) + part(z, 2),
                part(x, 1) + part(y, 3) + part(z, 4),
                part(x, 2) + part(y, 4) + part(z, 5),
            ],
            axis=0,
        )

    for wanted, row, start, step in ((within, 0, 0, 1), (beyond, 1, SLOTS - 1, -1)):
        if wanted:

            def several(at, carry):
                for k in range(GROUP):
                    add(start + step * (at * GROUP + k))
                return carry

            lax.fori_loop(0, lax.div(plan_ref[3, row] + (GROUP - 1), GROUP), several, 0)
    for i in range(tiles):
        out_ref[:, i * TILE : (i + 1) * TILE] = sum_ref[i]


def back_kernel(begin, factor_ref, before_ref, terms_ref, flip_ref, out_ref, left_ref):
    waves = left_ref.shape[2]
    particles = out_ref.shape[1]
    for i in range(waves // TILE):
        block = factor_ref[32 * i : 32 * i + 32, :]
        t = terms_ref[:, begin + i * TILE : begin + (i + 1) * TILE]
        block = block * t[0:1]
        for kind in range(2):
            one, two = block[16 * kind : 16 * kind + 8], block[16 * kind + 8 : 16 * kind + 16]
            rows = jnp.concatenate(
                [t[1:2] * one + t[3:4] * two, t[2:3] * one + t[4:5] * two, t[5:6] * two], axis=0
            )
            left_ref[kind, :, i * TILE : (i + 1) * TILE] = jnp.concatenate(split(rows), axis=0)
    step = min(512, particles)
    rows = slice(begin, begin + waves)
    for at in range(0, particles, step):
        cols = slice(at, at + step)
        total = before_ref[:, cols]
        for k in range(2):
            total = total + product(left_ref[k], flip_ref[k, rows, cols], flip_ref[2 + k, rows, cols])
        out_ref[:, cols] = total


def next_kernel(parts, share, *refs):
    ins, (force_ref, terms_ref, rows_ref, tiles_ref, norm_ref) = refs[:parts], refs[parts:]
    particles = force_ref.shape[1]
    total = ins[0][...]
    for ref in ins[1:]:
        total = total + ref[...]
    rows = force_ref[...] + total
    rows_ref[...] = rows
    tiles_ref[...] = own_tiles(rows, share, terms_ref[7:8, :TILE], particles // TILE // share)
    squares = rows * rows
    squares = squares[0:8] + squares[8:16] + squares[16:24]
    norm = squares[:, 0:TILE]
    for i in range(1, particles // TILE):
        norm = norm + squares[:, i * TILE : (i + 1) * TILE]
    norm_ref[...] = norm


def factor_kernel(rows_ref, tiles_ref, norm_ref, terms_ref, table_ref, mine_ref, rest_ref):
    base = mine_ref.shape[0]
    rest_ref[base : base + 8, :] = norm_ref[...]
    rest_ref[base + 8 :, :] = tiles_ref[...]
    forward(rows_ref[...], table_ref, terms_ref[...], mine_ref, rest_ref)


def final_kernel(parts, *refs):
    ins, (noise_ref, one_ref, two_ref, first_ref, second_ref, out_ref) = refs[:parts], refs[parts:]
    total = ins[0][...]
    for ref in ins[1:]:
        total = total + ref[...]
    u0, u1, u2 = noise_ref[...], one_ref[...], two_ref[...]
    u3 = u2 + total
    first = jnp.sum(first_ref[-8:, :], axis=1, keepdims=True)
    second = jnp.sum(second_ref[-8:, :], axis=1, keepdims=True)
    ratio = jnp.max(second / (first + EPSILON), axis=0, keepdims=True)
    high = SAFETY * jnp.sqrt(ratio)
    low = high / SPREAD
    nodes = DEGREE + 1
    angles = [math.pi * (j + 0.5) / nodes for j in range(nodes)]
    samples = [jnp.sqrt(0.5 * (high - low) * math.cos(t) + 0.5 * (high + low)) for t in angles]
    coeffs = []
    for k in range(nodes):
        acc = samples[0] * math.cos(k * angles[0])
        for j in range(1, nodes):
            acc = acc + samples[j] * math.cos(k * angles[j])
        coeffs.append(acc * (2.0 / nodes) * (0.5 if k == 0 else 1.0))
    p = 2.0 / (high - low)
    q = (high + low) / (high - low)
    v0, v1, v2 = p * u1 - q * u0, p * u2 - q * u1, p * u3 - q * u2
    t2 = 2.0 * (p * v1 - q * v0) - u0
    m2 = 2.0 * (p * v2 - q * v1) - u1
    t3 = 2.0 * (p * m2 - q * t2) - v0
    out_ref[...] = coeffs[0] * u0 + coeffs[1] * v0 + coeffs[2] * t2 + coeffs[3] * t3


def call(kernel, outs, args, scratch=(), smem_in=0, smem_out=(), flops=0, space=pltpu.VMEM):
    vmem = pl.BlockSpec(memory_space=pltpu.VMEM)
    smem = pl.BlockSpec(memory_space=pltpu.SMEM)
    return pl.pallas_call(
        kernel,
        out_shape=[jax.ShapeDtypeStruct(*o) for o in outs],
        in_specs=[smem] * smem_in + [pl.BlockSpec(memory_space=space)] * (len(args) - smem_in),
        out_specs=[smem if i in smem_out else vmem for i in range(len(outs))],
        scratch_shapes=list(scratch),
        cost_estimate=pl.CostEstimate(flops=flops, bytes_accessed=0, transcendentals=0),
        compiler_params=pltpu.CompilerParams(vmem_limit_bytes=VMEM_LIMIT),
    )(*args)


def exchange(x, axis, lowest):
    size = lax.axis_size(axis)
    bit = lowest
    parts = [x]
    while bit < size:
        if len(parts) > 1:
            x = functools.reduce(jnp.add, parts)
        radix = min(4, size // bit)
        parts = [x] + [
            lax.ppermute(x, axis, [(i, i ^ (d * bit)) for i in range(size)]) for d in ((2, 1, 3) if radix == 4 else range(1, radix))
        ]
        bit *= radix
    return parts


def body(noise, positions, wave_index, tile_lists, tile_counts):
    slabs = lax.axis_size("space")
    length_x = float(slabs)
    vectors = noise.shape[0]
    particles = positions.shape[1]
    waves = wave_index.shape[1]
    tiles = particles // TILE
    ranks = lax.axis_size("wave")
    share = tiles // ranks
    place = jnp.stack([lax.axis_index("space") & 1, lax.axis_index("wave")]).astype(jnp.int32)
    live = jnp.where(jnp.arange(NB_MOST)[None] < tile_counts[:, None], tile_lists, -1)
    core = [(i, i ^ 1) for i in range(slabs)]
    third = [(i, (i + 1 if i % 2 else i - 1) % slabs) for i in range(slabs)]
    table = ((4, particles, waves), BF16)
    rows_shape = ((3 * vectors, particles), F32)
    half = waves // TILE * 16
    base = half + 8
    far_flops = 2 * 96 * particles * waves * 2

    rows = jnp.transpose(noise, (1, 0, 2)).reshape(3 * vectors, particles)
    lines = jnp.broadcast_to(place.astype(F32)[:, None], (2, TILE))
    stack = jnp.concatenate([rows, positions], axis=0)
    phases, flipped, terms, mine, rest = call(
        functools.partial(start_kernel, length_x, share),
        [
            table,
            ((4, waves, particles), BF16),
            ((8, waves), F32),
            ((half, TILE), F32),
            ((base + 32 * share, TILE), F32),
        ],
        (wave_index, lines, stack),
        [
            pltpu.VMEM((particles, 16), BF16),
            pltpu.VMEM((6 * vectors, particles), BF16),
            pltpu.VMEM((2, 3 * vectors, waves), F32),
        ],
        flops=4 * far_flops,
    )
    noise_rows = rows
    images, norms = [], []

    matrices = plan = None
    for step in range(DEGREE):
        other = lax.ppermute(rest, "space", core)
        away = lax.ppermute(rest[base:] if step == 0 else own, "space", third)
        if step == 0:
            other, live = lax.optimization_barrier((other, live))
        chip = jnp.concatenate([mine, rest[half:base]], axis=0) + other[:base]
        parts = exchange(chip, "space", 2)
        if step == 0:
            matrices, plan = call(
                functools.partial(pair_kernel, length_x, base + 24 * share, share),
                [((SLOTS, 2 * TILE, 6 * TILE), BF16), ((4, SLOTS), jnp.int32)],
                (place, live, stack, rest, other, away),
                [pltpu.VMEM((tiles, 8, TILE), F32), pltpu.VMEM((3 * share, TILE, 8), F32)],
                smem_in=2,
                smem_out=(1,),
                flops=far_flops,
            )
        near_part = call(
            functools.partial(near_kernel, base, share, True, True),
            [rows_shape],
            (plan, rest, other, away, matrices),
            [pltpu.VMEM((3 * share, 24, TILE), F32), pltpu.VMEM((tiles + 1, 24, TILE), F32)],
            smem_in=1,
            flops=20 * far_flops,
        )[0]
        if step == 0:
            parts[-1], matrices = lax.optimization_barrier((parts[-1], matrices))
        else:
            parts[-1], near_part = lax.optimization_barrier((parts[-1], near_part))
        total = functools.reduce(jnp.add, parts)
        swapped = lax.ppermute(total[:half], "space", core)
        part = near_part
        for begin, factors in ((0, total), (waves // 2, swapped)):
            part = call(
                functools.partial(back_kernel, begin),
                [rows_shape],
                (factors, part, terms, flipped),
                [pltpu.VMEM((2, 6 * vectors, waves // 2), BF16)],
                flops=far_flops // 2,
            )[0]
        norms.append(total)
        sums = exchange(part, "wave", 1)
        if step < DEGREE - 1:
            rows, own, norm = call(
                functools.partial(next_kernel, len(sums), share),
                [rows_shape, ((24 * share, TILE), F32), ((8, TILE), F32)],
                (*sums, rows, terms),
                flops=1,
            )
            mine, rest = call(
                factor_kernel,
                [((half, TILE), F32), ((base + 24 * share, TILE), F32)],
                (rows, own, norm, terms, phases),
                flops=far_flops,
            )
            images.append(rows)
    out = call(
        functools.partial(final_kernel, len(sums)),
        [rows_shape],
        (*sums, noise_rows, *images, *norms[1:]),
    )[0]
    return jnp.transpose(out.reshape(3, vectors, particles), (1, 0, 2))


def solution(mesh):
    in_specs = (
        P(None, None, "space"),
        P(None, "space"),
        P(None, "wave"),
        P("space", None),
        P("space"),
    )
    out_specs = P(None, None, "space")
    return jax.shard_map(body, mesh=mesh, in_specs=in_specs, out_specs=out_specs, check_vma=False)
```

```python
import functools
import math

import jax
import jax.numpy as jnp
from jax import lax
from jax.experimental import pallas as pl
from jax.experimental.pallas import tpu as pltpu
from jax.sharding import PartitionSpec as P

TILE = 128
KW = 4096
NB_MOST = 8
DEGREE = 3
PAIR_MOST = 32
GROUP = 4
SLOTS = PAIR_MOST + GROUP

SIDE_CROSS = 8.0
NEAR_SQUARE = 0.36
NEAR_AMP = 0.15
FAR_AMP = 8.0
SPLIT_SQUARE = 64.0
SCREEN = 4.0
SAFETY = 1.25
SPREAD = 100.0
EPSILON = 1e-06

F32 = jnp.float32
BF16 = jnp.bfloat16
VMEM_LIMIT = 8 << 20

SINE = (4.44287968, -7.30781651, 3.59777427, -0.791199386)
ROUNDER = 12582912.0
COSINE = (1.4142040014266968, -6.97763729095459, 5.715188026428223, -1.728213906288147)


def split(x):
    high = x.astype(BF16)
    return high, (x - high.astype(F32)).astype(BF16)


def poly(coeffs, x):
    acc = coeffs[-1]
    for c in coeffs[-2::-1]:
        acc = acc * x + c
    return acc


def emit(kinds, terms, at, mine_ref, rest_ref):
    width = kinds[0].shape[1]
    t = terms[:, at : at + width]
    pieces = []
    for full in kinds:
        fx, fy, fz = full[0:8], full[8:16], full[16:24]
        pieces.append(t[1:2] * fx + t[2:3] * fy)
        pieces.append(t[3:4] * fx + t[4:5] * fy + t[5:6] * fz)
    stacked = jnp.concatenate(pieces, axis=0)
    half = mine_ref.shape[0]
    for k in range(width // TILE):
        row = (at // TILE + k) * 32
        ref, row = (mine_ref, row) if row < half else (rest_ref, row - half)
        ref[row : row + 32, :] = stacked[:, k * TILE : (k + 1) * TILE]


def product(both, high_table, low_table):
    first = jnp.dot(both, high_table, preferred_element_type=F32)
    second = jnp.dot(both[:24], low_table, preferred_element_type=F32)
    return first[:24] + (first[24:] + second)


def forward(rows, table_ref, terms, mine_ref, rest_ref):
    waves = table_ref.shape[2]
    both = jnp.concatenate(split(rows), axis=0)
    step = min(512, waves)
    for at in range(0, waves, step):
        cols = slice(at, at + step)
        kinds = [product(both, table_ref[k, :, cols], table_ref[2 + k, :, cols]) for k in range(2)]
        emit(kinds, terms, at, mine_ref, rest_ref)


def own_tiles(rows, share, rank, ranks):
    picked = []
    for k in range(share):
        tiles = [rows[:, t * TILE : (t + 1) * TILE] for t in range(k * ranks, (k + 1) * ranks)]
        mine = tiles[0]
        for r in range(1, ranks):
            mine = jnp.where(jnp.abs(rank - r) < 0.5, tiles[r], mine)
        picked.append(mine)
    return jnp.concatenate(picked, axis=0)


def start_kernel(
    length_x, share, index_ref, place_ref, stack_ref, table_ref, flip_ref, terms_ref, mine_ref, rest_ref,
    turn_ref, left_ref, sum_ref
):
    particles = table_ref.shape[1]
    waves = table_ref.shape[2]
    tiles = particles // TILE
    ranks = tiles // share
    sides = (length_x, SIDE_CROSS, SIDE_CROSS)
    core = place_ref[0:1]
    rank = place_ref[1:2]
    whole = index_ref[...].astype(F32)
    turned = jnp.concatenate([whole[:, waves // 2 :], whole[:, : waves // 2]], axis=1)
    first = jnp.broadcast_to(jnp.concatenate([core] * (waves // TILE), axis=1), whole.shape) < 0.5
    whole = jnp.where(first, whole, turned)
    counts = [whole[a : a + 1] for a in range(3)]
    k1, k2, k3 = [2.0 * math.pi * counts[a] / sides[a] for a in range(3)]
    square = k1 * k1 + k2 * k2 + k3 * k3
    scaled = square / SPLIT_SQUARE
    weight = FAR_AMP * (1.0 + scaled) * jnp.exp(-scaled) / (KW * (square + SCREEN))
    flat_square = k1 * k1 + k2 * k2
    flat = 1.0 / jnp.sqrt(flat_square)
    both = 1.0 / jnp.sqrt(square * flat_square)
    terms_ref[...] = jnp.concatenate(
        [
            weight,
            -k2 * flat,
            k1 * flat,
            -k1 * k3 * both,
            -k2 * k3 * both,
            flat_square * both,
            jnp.concatenate([place_ref[...]] * (waves // TILE), axis=1),
        ],
        axis=0,
    )
    noise = stack_ref[0:24, :particles]
    places = jnp.concatenate([stack_ref[24:27, :particles], jnp.zeros((5, particles), F32)], axis=0)
    base = waves // TILE * 16
    row = base + 8 + 24 * share
    rest_ref[base : base + 8, :] = jnp.zeros((8, TILE), F32)
    rest_ref[base + 8 : row, :] = own_tiles(noise, share, rank, ranks)
    rest_ref[row : row + 8 * share, :] = own_tiles(places, share, rank, ranks)
    left_ref[...] = jnp.concatenate(split(noise), axis=0)
    parts = []
    rest = jnp.concatenate([places[a : a + 1] / sides[a] for a in range(3)], axis=0)
    for _ in range(3):
        parts.append(rest.astype(BF16).astype(F32))
        rest = rest - parts[-1]
    turn_ref[...] = jnp.concatenate(parts + [jnp.zeros((7, particles), F32)], axis=0).T.astype(BF16)
    numbers = jnp.concatenate(counts * 3 + [jnp.zeros((7, waves), F32)], axis=0).astype(BF16)
    wide = 256

    def make(rows):
        for at in range(0, waves, wide):
            turns = jnp.dot(turn_ref[rows, :], numbers[:, at : at + wide], preferred_element_type=F32)
            for j in range(0, wide, TILE):
                cols = slice(at + j, at + j + TILE)
                t = turns[:, j : j + TILE]
                r = t - ((t + ROUNDER) - ROUNDER)
                x = r * r
                s = r * poly(SINE, x)
                c = poly(COSINE, x)
                table_ref[0, rows, cols], table_ref[2, rows, cols] = split(1.0 - s * s)
                table_ref[1, rows, cols], table_ref[3, rows, cols] = split(s * c)

    def use(rows, first):
        for kind in range(2):
            for at in range(0, waves, wide):
                cols = slice(at, at + wide)
                piece = product(left_ref[:, rows], table_ref[kind, rows, cols], table_ref[2 + kind, rows, cols])
                sum_ref[kind, :, cols] = piece if first else sum_ref[kind, :, cols] + piece
        for kind in range(4):
            flip_ref[kind, :, rows] = table_ref[kind, rows, :].T

    ends = [0] + [particles * k // 8 for k in (4, 6, 8)]
    blocks = [slice(low, high) for low, high in zip(ends, ends[1:])]
    make(blocks[0])
    for k in range(1, len(blocks)):
        use(blocks[k - 1], k == 1)
        make(blocks[k])
    use(blocks[-1], len(blocks) == 1)
    emit([sum_ref[0], sum_ref[1]], terms_ref[...], 0, mine_ref, rest_ref)


def fill_window(sources, share, window_ref):
    for slab, (ref, start) in enumerate(sources):
        for i in range(share):
            row = start + 24 * i
            window_ref[slab * share + i] = ref[row : row + 24, :]


def add_pair(target, source, matrix, sum_ref):
    high, low = split(source)
    left = jnp.concatenate(
        [
            jnp.concatenate([high, high], axis=1),
            jnp.concatenate([low, jnp.zeros_like(low)], axis=1),
        ],
        axis=0,
    )
    both = jnp.dot(left, matrix, preferred_element_type=F32)
    full = both[:24] + both[24:]
    x, y, z = full[0:8], full[8:16], full[16:24]

    def part(rows, at):
        return rows[:, at * TILE : (at + 1) * TILE]

    sum_ref[target] += jnp.concatenate(
        [
            part(x, 0) + part(y, 1) + part(z, 2),
            part(x, 1) + part(y, 3) + part(z, 4),
            part(x, 2) + part(y, 4) + part(z, 5),
        ],
        axis=0,
    )


def pair_kernel(
    length_x, base, share, live_ref, pos_ref, own_ref, near_ref, away_ref, out_ref, plan_ref, near_out_ref,
    place_ref, column_ref, window_ref, sum_ref
):
    tiles = pos_ref.shape[1] // TILE
    seen = jnp.int32(0)
    for target in range(tiles):
        for k in range(NB_MOST):
            code = live_ref[target, k]
            plan_ref[0, seen] = target
            plan_ref[1, seen] = code
            seen = seen + jnp.where(code >= 0, 1, 0)
    plan_ref[2, 0] = seen
    for k in range(GROUP):
        plan_ref[0, seen + k] = tiles
        plan_ref[1, seen + k] = 0
    fill_window(((own_ref, base), (near_ref, base), (away_ref, 0)), share, window_ref)
    sum_ref[...] = jnp.zeros_like(sum_ref)
    base = base + 24 * share
    sides = (length_x, SIDE_CROSS, SIDE_CROSS)
    reach = math.sqrt(NEAR_SQUARE)
    filler = jnp.zeros((5, TILE), F32)
    for i in range(tiles):
        lanes = slice(i * TILE, (i + 1) * TILE)
        place_ref[i] = jnp.concatenate([pos_ref[24 + a : 25 + a, lanes] / sides[a] for a in range(3)] + [filler], axis=0)
    for slab, ref in enumerate((own_ref, near_ref, away_ref)):
        for i in range(share):
            row = (base if slab < 2 else 24 * share) + 8 * i
            place = ref[row : row + 8, :]
            place = jnp.concatenate([place[a : a + 1] / sides[a] for a in range(3)] + [filler], axis=0)
            column_ref[slab * share + i] = place.T
    count = 32

    def pair(p, carry):
        q = jnp.maximum(p - 1, 0)
        add_pair(
            jnp.where(p == 0, tiles, plan_ref[0, q]), window_ref[plan_ref[1, q] >> 1], out_ref[q], sum_ref
        )
        target = place_ref[plan_ref[0, p]]
        source = column_ref[plan_ref[1, p] >> 1]
        own = (plan_ref[1, p] & 1).astype(F32)
        lines = [target[a : a + 1] for a in range(3)]
        for low in range(0, TILE, count):
            rows = slice(low, low + count)
            q = []
            for a in range(3):
                offset = lines[a] - jnp.broadcast_to(source[rows, a : a + 1], (count, TILE))
                offset = offset - jnp.floor(offset + 0.5)
                q.append(offset * (sides[a] / reach))
            square = q[0] * q[0] + q[1] * q[1] + q[2] * q[2]
            same = (
                lax.broadcasted_iota(jnp.int32, (count, TILE), 0) + low
                == lax.broadcasted_iota(jnp.int32, (count, TILE), 1)
            )
            envelope = jnp.exp(-square) * jnp.where(same, NEAR_AMP * (1.0 - own), NEAR_AMP)
            slot = 0
            for a in range(3):
                scaled = envelope * q[a]
                for b in range(a, 3):
                    value = scaled * q[b]
                    if a == b:
                        value = value + envelope
                    cols = slice(slot * TILE, (slot + 1) * TILE)
                    out_ref[p, rows, cols], out_ref[p, TILE + low : TILE + low + count, cols] = split(value)
                    slot += 1
        return carry

    lax.fori_loop(0, seen + 1, pair, 0)
    for i in range(tiles):
        near_out_ref[:, i * TILE : (i + 1) * TILE] = sum_ref[i]


def near_kernel(base, share, plan_ref, own_ref, near_ref, away_ref, matrix_ref, out_ref, window_ref, sum_ref):
    fill_window(((own_ref, base), (near_ref, base), (away_ref, 0)), share, window_ref)
    sum_ref[...] = jnp.zeros_like(sum_ref)

    def several(at, carry):
        for k in range(GROUP):
            p = at * GROUP + k
            add_pair(plan_ref[0, p], window_ref[plan_ref[1, p] >> 1], matrix_ref[p], sum_ref)
        return carry

    lax.fori_loop(0, lax.div(plan_ref[2, 0] + (GROUP - 1), GROUP), several, 0)
    for i in range(sum_ref.shape[0] - 1):
        out_ref[:, i * TILE : (i + 1) * TILE] = sum_ref[i]


def back_kernel(begin, factor_ref, before_ref, terms_ref, flip_ref, out_ref, left_ref):
    waves = left_ref.shape[2]
    particles = out_ref.shape[1]
    for i in range(waves // TILE):
        block = factor_ref[32 * i : 32 * i + 32, :]
        t = terms_ref[:, begin + i * TILE : begin + (i + 1) * TILE]
        block = block * t[0:1]
        for kind in range(2):
            one, two = block[16 * kind : 16 * kind + 8], block[16 * kind + 8 : 16 * kind + 16]
            rows = jnp.concatenate(
                [t[1:2] * one + t[3:4] * two, t[2:3] * one + t[4:5] * two, t[5:6] * two], axis=0
            )
            left_ref[kind, :, i * TILE : (i + 1) * TILE] = jnp.concatenate(split(rows), axis=0)
    step = min(512, particles)
    rows = slice(begin, begin + waves)
    for at in range(0, particles, step):
        cols = slice(at, at + step)
        total = before_ref[:, cols]
        for k in range(2):
            total = total + product(left_ref[k], flip_ref[k, rows, cols], flip_ref[2 + k, rows, cols])
        out_ref[:, cols] = total


def next_kernel(parts, share, *refs):
    ins, (force_ref, terms_ref, rows_ref, tiles_ref, norm_ref) = refs[:parts], refs[parts:]
    particles = force_ref.shape[1]
    total = ins[0][...]
    for ref in ins[1:]:
        total = total + ref[...]
    rows = force_ref[...] + total
    rows_ref[...] = rows
    tiles_ref[...] = own_tiles(rows, share, terms_ref[7:8, :TILE], particles // TILE // share)
    squares = rows * rows
    squares = squares[0:8] + squares[8:16] + squares[16:24]
    norm = squares[:, 0:TILE]
    for i in range(1, particles // TILE):
        norm = norm + squares[:, i * TILE : (i + 1) * TILE]
    norm_ref[...] = norm


def factor_kernel(rows_ref, tiles_ref, norm_ref, terms_ref, table_ref, mine_ref, rest_ref):
    base = mine_ref.shape[0]
    rest_ref[base : base + 8, :] = norm_ref[...]
    rest_ref[base + 8 :, :] = tiles_ref[...]
    forward(rows_ref[...], table_ref, terms_ref[...], mine_ref, rest_ref)


def final_kernel(parts, *refs):
    ins, (noise_ref, one_ref, two_ref, first_ref, second_ref, out_ref) = refs[:parts], refs[parts:]
    total = ins[0][...]
    for ref in ins[1:]:
        total = total + ref[...]
    u0, u1, u2 = noise_ref[...], one_ref[...], two_ref[...]
    u3 = u2 + total
    first = jnp.sum(first_ref[-8:, :], axis=1, keepdims=True)
    second = jnp.sum(second_ref[-8:, :], axis=1, keepdims=True)
    ratio = jnp.max(second / (first + EPSILON), axis=0, keepdims=True)
    high = SAFETY * jnp.sqrt(ratio)
    low = high / SPREAD
    nodes = DEGREE + 1
    angles = [math.pi * (j + 0.5) / nodes for j in range(nodes)]
    samples = [jnp.sqrt(0.5 * (high - low) * math.cos(t) + 0.5 * (high + low)) for t in angles]
    coeffs = []
    for k in range(nodes):
        acc = samples[0] * math.cos(k * angles[0])
        for j in range(1, nodes):
            acc = acc + samples[j] * math.cos(k * angles[j])
        coeffs.append(acc * (2.0 / nodes) * (0.5 if k == 0 else 1.0))
    p = 2.0 / (high - low)
    q = (high + low) / (high - low)
    v0, v1, v2 = p * u1 - q * u0, p * u2 - q * u1, p * u3 - q * u2
    t2 = 2.0 * (p * v1 - q * v0) - u0
    m2 = 2.0 * (p * v2 - q * v1) - u1
    t3 = 2.0 * (p * m2 - q * t2) - v0
    out_ref[...] = coeffs[0] * u0 + coeffs[1] * v0 + coeffs[2] * t2 + coeffs[3] * t3


def call(kernel, outs, args, scratch=(), smem_in=0, smem_out=(), flops=0, space=pltpu.VMEM):
    vmem = pl.BlockSpec(memory_space=pltpu.VMEM)
    smem = pl.BlockSpec(memory_space=pltpu.SMEM)
    return pl.pallas_call(
        kernel,
        out_shape=[jax.ShapeDtypeStruct(*o) for o in outs],
        in_specs=[smem] * smem_in + [pl.BlockSpec(memory_space=space)] * (len(args) - smem_in),
        out_specs=[smem if i in smem_out else vmem for i in range(len(outs))],
        scratch_shapes=list(scratch),
        cost_estimate=pl.CostEstimate(flops=flops, bytes_accessed=0, transcendentals=0),
        compiler_params=pltpu.CompilerParams(vmem_limit_bytes=VMEM_LIMIT),
    )(*args)


def exchange(x, axis, lowest):
    size = lax.axis_size(axis)
    bit = lowest
    parts = [x]
    while bit < size:
        if len(parts) > 1:
            x = functools.reduce(jnp.add, parts)
        radix = min(4, size // bit)
        parts = [x] + [
            lax.ppermute(x, axis, [(i, i ^ (d * bit)) for i in range(size)]) for d in ((2, 1, 3) if radix == 4 else range(1, radix))
        ]
        bit *= radix
    return parts


def body(noise, positions, wave_index, tile_lists, tile_counts):
    slabs = lax.axis_size("space")
    length_x = float(slabs)
    vectors = noise.shape[0]
    particles = positions.shape[1]
    waves = wave_index.shape[1]
    tiles = particles // TILE
    ranks = lax.axis_size("wave")
    share = tiles // ranks
    place = jnp.stack([lax.axis_index("space") & 1, lax.axis_index("wave")]).astype(jnp.int32)
    core = [(i, i ^ 1) for i in range(slabs)]
    third = [(i, (i + 1 if i % 2 else i - 1) % slabs) for i in range(slabs)]
    table = ((4, particles, waves), BF16)
    rows_shape = ((3 * vectors, particles), F32)
    half = waves // TILE * 16
    base = half + 8
    far_flops = 2 * 96 * particles * waves * 2

    rows = jnp.transpose(noise, (1, 0, 2)).reshape(3 * vectors, particles)
    lines = jnp.broadcast_to(place.astype(F32)[:, None], (2, TILE))
    stack = jnp.concatenate([rows, positions], axis=0)
    phases, flipped, terms, mine, rest = call(
        functools.partial(start_kernel, length_x, share),
        [
            table,
            ((4, waves, particles), BF16),
            ((8, waves), F32),
            ((half, TILE), F32),
            ((base + 32 * share, TILE), F32),
        ],
        (wave_index, lines, stack),
        [
            pltpu.VMEM((particles, 16), BF16),
            pltpu.VMEM((6 * vectors, particles), BF16),
            pltpu.VMEM((2, 3 * vectors, waves), F32),
        ],
        flops=4 * far_flops,
    )
    core_line = jnp.broadcast_to(terms[6:7, :NB_MOST], tile_lists.shape)
    rank_line = jnp.broadcast_to(terms[7:8, :NB_MOST], tile_lists.shape)
    side, tile = tile_lists // tiles, tile_lists % tiles
    which = jnp.where(side == 1, 0, jnp.where((side == 0) == (core_line > 0.5), 1, 2))
    targets = lax.broadcasted_iota(jnp.int32, tile_lists.shape, 0)
    slots = lax.broadcasted_iota(jnp.int32, tile_lists.shape, 1)
    itself = tile_lists - targets == tiles
    code = 2 * (which * share + tile // ranks) + itself.astype(jnp.int32)
    wanted = (slots < tile_counts[:, None]) & (tile % ranks == rank_line.astype(jnp.int32))
    live = jnp.where(wanted, code, -1)
    noise_rows = rows
    images, norms = [], []

    matrices = plan = None
    for step in range(DEGREE):
        other = lax.ppermute(rest, "space", core)
        away = lax.ppermute(rest[base:] if step == 0 else own, "space", third)
        if step == 0:
            other, live = lax.optimization_barrier((other, live))
        chip = jnp.concatenate([mine, rest[half:base]], axis=0) + other[:base]
        parts = exchange(chip, "space", 2)
        window = [pltpu.VMEM((3 * share, 24, TILE), F32), pltpu.VMEM((tiles + 1, 24, TILE), F32)]
        if step == 0:
            matrices, plan, near_part = call(
                functools.partial(pair_kernel, length_x, base, share),
                [((SLOTS, 2 * TILE, 6 * TILE), BF16), ((3, SLOTS), jnp.int32), rows_shape],
                (live, stack, rest, other, away),
                [pltpu.VMEM((tiles + 1, 8, TILE), F32), pltpu.VMEM((3 * share, TILE, 8), F32), *window],
                smem_in=1,
                smem_out=(1,),
                flops=20 * far_flops,
            )
        else:
            near_part = call(
                functools.partial(near_kernel, base, share),
                [rows_shape],
                (plan, rest, other, away, matrices),
                window,
                smem_in=1,
                flops=20 * far_flops,
            )[0]
        parts[-1], near_part = lax.optimization_barrier((parts[-1], near_part))
        total = functools.reduce(jnp.add, parts)
        swapped = lax.ppermute(total[:half], "space", core)
        part = near_part
        for begin, factors in ((0, total), (waves // 2, swapped)):
            part = call(
                functools.partial(back_kernel, begin),
                [rows_shape],
                (factors, part, terms, flipped),
                [pltpu.VMEM((2, 6 * vectors, waves // 2), BF16)],
                flops=far_flops // 2,
            )[0]
        norms.append(total)
        sums = exchange(part, "wave", 1)
        if step < DEGREE - 1:
            rows, own, norm = call(
                functools.partial(next_kernel, len(sums), share),
                [rows_shape, ((24 * share, TILE), F32), ((8, TILE), F32)],
                (*sums, rows, terms),
                flops=1,
            )
            mine, rest = call(
                factor_kernel,
                [((half, TILE), F32), ((base + 24 * share, TILE), F32)],
                (rows, own, norm, terms, phases),
                flops=far_flops,
            )
            images.append(rows)
    out = call(
        functools.partial(final_kernel, len(sums)),
        [rows_shape],
        (*sums, noise_rows, *images, *norms[1:]),
    )[0]
    return jnp.transpose(out.reshape(3, vectors, particles), (1, 0, 2))


def solution(mesh):
    in_specs = (
        P(None, None, "space"),
        P(None, "space"),
        P(None, "wave"),
        P("space", None),
        P("space"),
    )
    out_specs = P(None, None, "space")
    return jax.shard_map(body, mesh=mesh, in_specs=in_specs, out_specs=out_specs, check_vma=False)
```

```python
import functools
import math

import jax
import jax.numpy as jnp
from jax import lax
from jax.experimental import pallas as pl
from jax.experimental.pallas import tpu as pltpu
from jax.sharding import PartitionSpec as P

TILE = 128
KW = 4096
NB_MOST = 8
DEGREE = 3
PAIR_MOST = 32
GROUP = 4
SLOTS = PAIR_MOST + GROUP

SIDE_CROSS = 8.0
NEAR_SQUARE = 0.36
NEAR_AMP = 0.15
FAR_AMP = 8.0
SPLIT_SQUARE = 64.0
SCREEN = 4.0
SAFETY = 1.25
SPREAD = 100.0
EPSILON = 1e-06

F32 = jnp.float32
BF16 = jnp.bfloat16
VMEM_LIMIT = 8 << 20

SINE = (4.44287968, -7.30781651, 3.59777427, -0.791199386)
ROUNDER = 12582912.0
COSINE = (1.4142040014266968, -6.97763729095459, 5.715188026428223, -1.728213906288147)


def split(x):
    high = x.astype(BF16)
    return high, (x - high.astype(F32)).astype(BF16)


def poly(coeffs, x):
    acc = coeffs[-1]
    for c in coeffs[-2::-1]:
        acc = acc * x + c
    return acc


def emit(kinds, terms, at, mine_ref, rest_ref):
    width = kinds[0].shape[1]
    t = terms[:, at : at + width]
    pieces = []
    for full in kinds:
        fx, fy, fz = full[0:8], full[8:16], full[16:24]
        pieces.append(t[1:2] * fx + t[2:3] * fy)
        pieces.append(t[3:4] * fx + t[4:5] * fy + t[5:6] * fz)
    stacked = jnp.concatenate(pieces, axis=0)
    half = mine_ref.shape[0]
    for k in range(width // TILE):
        row = (at // TILE + k) * 32
        ref, row = (mine_ref, row) if row < half else (rest_ref, row - half)
        ref[row : row + 32, :] = stacked[:, k * TILE : (k + 1) * TILE]


def product(both, high_table, low_table):
    first = jnp.dot(both, high_table, preferred_element_type=F32)
    second = jnp.dot(both[:24], low_table, preferred_element_type=F32)
    return first[:24] + (first[24:] + second)


def forward(rows, table_ref, terms, mine_ref, rest_ref):
    waves = table_ref.shape[2]
    both = jnp.concatenate(split(rows), axis=0)
    step = min(512, waves)
    for at in range(0, waves, step):
        cols = slice(at, at + step)
        kinds = [product(both, table_ref[k, :, cols], table_ref[2 + k, :, cols]) for k in range(2)]
        emit(kinds, terms, at, mine_ref, rest_ref)


def own_tiles(rows, share, rank, ranks):
    picked = []
    for k in range(share):
        tiles = [rows[:, t * TILE : (t + 1) * TILE] for t in range(k * ranks, (k + 1) * ranks)]
        mine = tiles[0]
        for r in range(1, ranks):
            mine = jnp.where(jnp.abs(rank - r) < 0.5, tiles[r], mine)
        picked.append(mine)
    return jnp.concatenate(picked, axis=0)


def start_kernel(
    length_x, share, index_ref, place_ref, stack_ref, table_ref, flip_ref, terms_ref, mine_ref, rest_ref,
    turn_ref, left_ref, sum_ref
):
    particles = table_ref.shape[1]
    waves = table_ref.shape[2]
    tiles = particles // TILE
    ranks = tiles // share
    sides = (length_x, SIDE_CROSS, SIDE_CROSS)
    core = place_ref[0:1]
    rank = place_ref[1:2]
    whole = index_ref[...].astype(F32)
    turned = jnp.concatenate([whole[:, waves // 2 :], whole[:, : waves // 2]], axis=1)
    first = jnp.broadcast_to(jnp.concatenate([core] * (waves // TILE), axis=1), whole.shape) < 0.5
    whole = jnp.where(first, whole, turned)
    counts = [whole[a : a + 1] for a in range(3)]
    k1, k2, k3 = [2.0 * math.pi * counts[a] / sides[a] for a in range(3)]
    square = k1 * k1 + k2 * k2 + k3 * k3
    scaled = square / SPLIT_SQUARE
    weight = FAR_AMP * (1.0 + scaled) * jnp.exp(-scaled) / (KW * (square + SCREEN))
    flat_square = k1 * k1 + k2 * k2
    flat = 1.0 / jnp.sqrt(flat_square)
    both = 1.0 / jnp.sqrt(square * flat_square)
    terms_ref[...] = jnp.concatenate(
        [
            weight,
            -k2 * flat,
            k1 * flat,
            -k1 * k3 * both,
            -k2 * k3 * both,
            flat_square * both,
            jnp.concatenate([place_ref[...]] * (waves // TILE), axis=1),
        ],
        axis=0,
    )
    noise = stack_ref[0:24, :particles]
    places = jnp.concatenate([stack_ref[24:27, :particles], jnp.zeros((5, particles), F32)], axis=0)
    base = waves // TILE * 16
    row = base + 8 + 24 * share
    rest_ref[base : base + 8, :] = jnp.zeros((8, TILE), F32)
    rest_ref[base + 8 : row, :] = own_tiles(noise, share, rank, ranks)
    rest_ref[row : row + 8 * share, :] = own_tiles(places, share, rank, ranks)
    left_ref[...] = jnp.concatenate(split(noise), axis=0)
    parts = []
    rest = jnp.concatenate([places[a : a + 1] / sides[a] for a in range(3)], axis=0)
    for _ in range(3):
        parts.append(rest.astype(BF16).astype(F32))
        rest = rest - parts[-1]
    turn_ref[...] = jnp.concatenate(parts + [jnp.zeros((7, particles), F32)], axis=0).T.astype(BF16)
    numbers = jnp.concatenate(counts * 3 + [jnp.zeros((7, waves), F32)], axis=0).astype(BF16)
    wide = 256

    def make(rows):
        for at in range(0, waves, wide):
            turns = jnp.dot(turn_ref[rows, :], numbers[:, at : at + wide], preferred_element_type=F32)
            for j in range(0, wide, TILE):
                cols = slice(at + j, at + j + TILE)
                t = turns[:, j : j + TILE]
                r = t - ((t + ROUNDER) - ROUNDER)
                x = r * r
                s = r * poly(SINE, x)
                c = poly(COSINE, x)
                table_ref[0, rows, cols], table_ref[2, rows, cols] = split(1.0 - s * s)
                table_ref[1, rows, cols], table_ref[3, rows, cols] = split(s * c)

    def use(rows, first):
        for kind in range(2):
            for at in range(0, waves, wide):
                cols = slice(at, at + wide)
                piece = product(left_ref[:, rows], table_ref[kind, rows, cols], table_ref[2 + kind, rows, cols])
                sum_ref[kind, :, cols] = piece if first else sum_ref[kind, :, cols] + piece
        for kind in range(4):
            flip_ref[kind, :, rows] = table_ref[kind, rows, :].T

    ends = [0] + [particles * k // 8 for k in (4, 6, 8)]
    blocks = [slice(low, high) for low, high in zip(ends, ends[1:])]
    make(blocks[0])
    for k in range(1, len(blocks)):
        use(blocks[k - 1], k == 1)
        make(blocks[k])
    use(blocks[-1], len(blocks) == 1)
    emit([sum_ref[0], sum_ref[1]], terms_ref[...], 0, mine_ref, rest_ref)


def fill_window(sources, share, window_ref):
    for slab, (ref, start) in enumerate(sources):
        for i in range(share):
            row = start + 24 * i
            window_ref[slab * share + i] = ref[row : row + 24, :]


def add_pair(target, source, matrix, sum_ref):
    high, low = split(source)
    left = jnp.concatenate(
        [
            jnp.concatenate([high, high], axis=1),
            jnp.concatenate([low, jnp.zeros_like(low)], axis=1),
        ],
        axis=0,
    )
    both = jnp.dot(left, matrix, preferred_element_type=F32)
    full = both[:24] + both[24:]
    x, y, z = full[0:8], full[8:16], full[16:24]

    def part(rows, at):
        return rows[:, at * TILE : (at + 1) * TILE]

    sum_ref[target] += jnp.concatenate(
        [
            part(x, 0) + part(y, 1) + part(z, 2),
            part(x, 1) + part(y, 3) + part(z, 4),
            part(x, 2) + part(y, 4) + part(z, 5),
        ],
        axis=0,
    )


def pair_kernel(
    length_x, base, share, live_ref, pos_ref, own_ref, near_ref, away_ref, out_ref, plan_ref, near_out_ref,
    place_ref, column_ref, window_ref, sum_ref
):
    tiles = pos_ref.shape[1] // TILE
    seen = jnp.int32(0)
    for target in range(tiles):
        for k in range(NB_MOST):
            code = live_ref[target, k]
            plan_ref[0, seen] = target
            plan_ref[1, seen] = code
            seen = seen + jnp.where(code >= 0, 1, 0)
    plan_ref[2, 0] = seen
    for k in range(GROUP):
        plan_ref[0, seen + k] = tiles
        plan_ref[1, seen + k] = 0
    fill_window(((own_ref, base), (near_ref, base), (away_ref, 0)), share, window_ref)
    sum_ref[...] = jnp.zeros_like(sum_ref)
    base = base + 24 * share
    sides = (length_x, SIDE_CROSS, SIDE_CROSS)
    reach = math.sqrt(NEAR_SQUARE)
    filler = jnp.zeros((5, TILE), F32)
    for i in range(tiles):
        lanes = slice(i * TILE, (i + 1) * TILE)
        place_ref[i] = jnp.concatenate([pos_ref[24 + a : 25 + a, lanes] / sides[a] for a in range(3)] + [filler], axis=0)
    for slab, ref in enumerate((own_ref, near_ref, away_ref)):
        for i in range(share):
            row = (base if slab < 2 else 24 * share) + 8 * i
            place = ref[row : row + 8, :]
            place = jnp.concatenate([place[a : a + 1] / sides[a] for a in range(3)] + [filler], axis=0)
            column_ref[slab * share + i] = place.T
    count = 32

    def pair(p, carry):
        q = jnp.maximum(p - 1, 0)
        add_pair(
            jnp.where(p == 0, tiles, plan_ref[0, q]), window_ref[plan_ref[1, q] >> 1], out_ref[q], sum_ref
        )
        target = place_ref[plan_ref[0, p]]
        source = column_ref[plan_ref[1, p] >> 1]
        own = (plan_ref[1, p] & 1).astype(F32)
        lines = [target[a : a + 1] for a in range(3)]
        for low in range(0, TILE, count):
            rows = slice(low, low + count)
            q = []
            for a in range(3):
                offset = lines[a] - jnp.broadcast_to(source[rows, a : a + 1], (count, TILE))
                offset = offset - jnp.floor(offset + 0.5)
                q.append(offset * (sides[a] / reach))
            square = q[0] * q[0] + q[1] * q[1] + q[2] * q[2]
            same = (
                lax.broadcasted_iota(jnp.int32, (count, TILE), 0) + low
                == lax.broadcasted_iota(jnp.int32, (count, TILE), 1)
            )
            envelope = jnp.exp(-square) * jnp.where(same, NEAR_AMP * (1.0 - own), NEAR_AMP)
            slot = 0
            for a in range(3):
                scaled = envelope * q[a]
                for b in range(a, 3):
                    value = scaled * q[b]
                    if a == b:
                        value = value + envelope
                    cols = slice(slot * TILE, (slot + 1) * TILE)
                    out_ref[p, rows, cols], out_ref[p, TILE + low : TILE + low + count, cols] = split(value)
                    slot += 1
        return carry

    lax.fori_loop(0, seen + 1, pair, 0)
    for i in range(tiles):
        near_out_ref[:, i * TILE : (i + 1) * TILE] = sum_ref[i]


def near_kernel(base, share, plan_ref, own_ref, near_ref, away_ref, matrix_ref, out_ref, window_ref, sum_ref):
    fill_window(((own_ref, base), (near_ref, base), (away_ref, 0)), share, window_ref)
    sum_ref[...] = jnp.zeros_like(sum_ref)

    def several(at, carry):
        for k in range(GROUP):
            p = at * GROUP + k
            add_pair(plan_ref[0, p], window_ref[plan_ref[1, p] >> 1], matrix_ref[p], sum_ref)
        return carry

    lax.fori_loop(0, lax.div(plan_ref[2, 0] + (GROUP - 1), GROUP), several, 0)
    for i in range(sum_ref.shape[0] - 1):
        out_ref[:, i * TILE : (i + 1) * TILE] = sum_ref[i]


def back_kernel(begin, factor_ref, before_ref, terms_ref, flip_ref, out_ref, left_ref):
    waves = left_ref.shape[2]
    particles = out_ref.shape[1]
    for i in range(waves // TILE):
        block = factor_ref[32 * i : 32 * i + 32, :]
        t = terms_ref[:, begin + i * TILE : begin + (i + 1) * TILE]
        block = block * t[0:1]
        for kind in range(2):
            one, two = block[16 * kind : 16 * kind + 8], block[16 * kind + 8 : 16 * kind + 16]
            rows = jnp.concatenate(
                [t[1:2] * one + t[3:4] * two, t[2:3] * one + t[4:5] * two, t[5:6] * two], axis=0
            )
            left_ref[kind, :, i * TILE : (i + 1) * TILE] = jnp.concatenate(split(rows), axis=0)
    step = min(512, particles)
    rows = slice(begin, begin + waves)
    for at in range(0, particles, step):
        cols = slice(at, at + step)
        total = before_ref[:, cols]
        for k in range(2):
            total = total + product(left_ref[k], flip_ref[k, rows, cols], flip_ref[2 + k, rows, cols])
        out_ref[:, cols] = total


def next_kernel(parts, share, *refs):
    ins, (force_ref, terms_ref, rows_ref, tiles_ref, norm_ref) = refs[:parts], refs[parts:]
    particles = force_ref.shape[1]
    total = ins[0][...]
    for ref in ins[1:]:
        total = total + ref[...]
    rows = force_ref[...] + total
    rows_ref[...] = rows
    tiles_ref[...] = own_tiles(rows, share, terms_ref[7:8, :TILE], particles // TILE // share)
    squares = rows * rows
    squares = squares[0:8] + squares[8:16] + squares[16:24]
    norm = squares[:, 0:TILE]
    for i in range(1, particles // TILE):
        norm = norm + squares[:, i * TILE : (i + 1) * TILE]
    norm_ref[...] = norm


def factor_kernel(rows_ref, tiles_ref, norm_ref, terms_ref, table_ref, mine_ref, rest_ref):
    base = mine_ref.shape[0]
    rest_ref[base : base + 8, :] = norm_ref[...]
    rest_ref[base + 8 :, :] = tiles_ref[...]
    forward(rows_ref[...], table_ref, terms_ref[...], mine_ref, rest_ref)


def series_kernel(noise_ref, one_ref, two_ref, first_ref, second_ref, base_ref, scale_ref):
    u0, u1, u2 = noise_ref[...], one_ref[...], two_ref[...]
    first = jnp.sum(first_ref[-8:, :], axis=1, keepdims=True)
    second = jnp.sum(second_ref[-8:, :], axis=1, keepdims=True)
    ratio = jnp.max(second / (first + EPSILON), axis=0, keepdims=True)
    high = SAFETY * jnp.sqrt(ratio)
    low = high / SPREAD
    nodes = DEGREE + 1
    angles = [math.pi * (j + 0.5) / nodes for j in range(nodes)]
    samples = [jnp.sqrt(0.5 * (high - low) * math.cos(t) + 0.5 * (high + low)) for t in angles]
    coeffs = []
    for k in range(nodes):
        acc = samples[0] * math.cos(k * angles[0])
        for j in range(1, nodes):
            acc = acc + samples[j] * math.cos(k * angles[j])
        coeffs.append(acc * (2.0 / nodes) * (0.5 if k == 0 else 1.0))
    p = 2.0 / (high - low)
    q = (high + low) / (high - low)
    v0, v1, v2 = p * u1 - q * u0, p * u2 - q * u1, p * u2 - q * u2
    t2 = 2.0 * (p * v1 - q * v0) - u0
    m2 = 2.0 * (p * v2 - q * v1) - u1
    t3 = 2.0 * (p * m2 - q * t2) - v0
    base_ref[...] = coeffs[0] * u0 + coeffs[1] * v0 + coeffs[2] * t2 + coeffs[3] * t3
    scale_ref[0:8, :] = jnp.broadcast_to(p, (8, TILE))
    scale_ref[8:16, :] = jnp.broadcast_to(coeffs[3], (8, TILE))


def final_kernel(parts, *refs):
    ins, (base_ref, scale_ref, out_ref) = refs[:parts], refs[parts:]
    total = ins[0][...]
    for ref in ins[1:]:
        total = total + ref[...]
    p, last = scale_ref[0:1, 0:1], scale_ref[8:9, 0:1]
    out_ref[...] = base_ref[...] + last * (2.0 * p * (2.0 * p * (p * total)))


def call(kernel, outs, args, scratch=(), smem_in=0, smem_out=(), flops=0, space=pltpu.VMEM):
    vmem = pl.BlockSpec(memory_space=pltpu.VMEM)
    smem = pl.BlockSpec(memory_space=pltpu.SMEM)
    return pl.pallas_call(
        kernel,
        out_shape=[jax.ShapeDtypeStruct(*o) for o in outs],
        in_specs=[smem] * smem_in + [pl.BlockSpec(memory_space=space)] * (len(args) - smem_in),
        out_specs=[smem if i in smem_out else vmem for i in range(len(outs))],
        scratch_shapes=list(scratch),
        cost_estimate=pl.CostEstimate(flops=flops, bytes_accessed=0, transcendentals=0),
        compiler_params=pltpu.CompilerParams(vmem_limit_bytes=VMEM_LIMIT),
    )(*args)


def exchange(x, axis, lowest):
    size = lax.axis_size(axis)
    bit = lowest
    parts = [x]
    while bit < size:
        if len(parts) > 1:
            x = functools.reduce(jnp.add, parts)
        radix = min(4, size // bit)
        parts = [x] + [
            lax.ppermute(x, axis, [(i, i ^ (d * bit)) for i in range(size)]) for d in ((2, 1, 3) if radix == 4 else range(1, radix))
        ]
        bit *= radix
    return parts


def body(noise, positions, wave_index, tile_lists, tile_counts):
    slabs = lax.axis_size("space")
    length_x = float(slabs)
    vectors = noise.shape[0]
    particles = positions.shape[1]
    waves = wave_index.shape[1]
    tiles = particles // TILE
    ranks = lax.axis_size("wave")
    share = tiles // ranks
    place = jnp.stack([lax.axis_index("space") & 1, lax.axis_index("wave")]).astype(jnp.int32)
    core = [(i, i ^ 1) for i in range(slabs)]
    third = [(i, (i + 1 if i % 2 else i - 1) % slabs) for i in range(slabs)]
    table = ((4, particles, waves), BF16)
    rows_shape = ((3 * vectors, particles), F32)
    half = waves // TILE * 16
    base = half + 8
    far_flops = 2 * 96 * particles * waves * 2

    rows = jnp.transpose(noise, (1, 0, 2)).reshape(3 * vectors, particles)
    lines = jnp.broadcast_to(place.astype(F32)[:, None], (2, TILE))
    stack = jnp.concatenate([rows, positions], axis=0)
    phases, flipped, terms, mine, rest = call(
        functools.partial(start_kernel, length_x, share),
        [
            table,
            ((4, waves, particles), BF16),
            ((8, waves), F32),
            ((half, TILE), F32),
            ((base + 32 * share, TILE), F32),
        ],
        (wave_index, lines, stack),
        [
            pltpu.VMEM((particles, 16), BF16),
            pltpu.VMEM((6 * vectors, particles), BF16),
            pltpu.VMEM((2, 3 * vectors, waves), F32),
        ],
        flops=4 * far_flops,
    )
    core_line = jnp.broadcast_to(terms[6:7, :NB_MOST], tile_lists.shape)
    rank_line = jnp.broadcast_to(terms[7:8, :NB_MOST], tile_lists.shape)
    side, tile = tile_lists // tiles, tile_lists % tiles
    which = jnp.where(side == 1, 0, jnp.where((side == 0) == (core_line > 0.5), 1, 2))
    targets = lax.broadcasted_iota(jnp.int32, tile_lists.shape, 0)
    slots = lax.broadcasted_iota(jnp.int32, tile_lists.shape, 1)
    itself = tile_lists - targets == tiles
    code = 2 * (which * share + tile // ranks) + itself.astype(jnp.int32)
    wanted = (slots < tile_counts[:, None]) & (tile % ranks == rank_line.astype(jnp.int32))
    live = jnp.where(wanted, code, -1)
    noise_rows = rows
    images, norms = [], []

    matrices = plan = None
    for step in range(DEGREE):
        other = lax.ppermute(rest, "space", core)
        away = lax.ppermute(rest[base:] if step == 0 else own, "space", third)
        if step == 0:
            other, live = lax.optimization_barrier((other, live))
        chip = jnp.concatenate([mine, rest[half:base]], axis=0) + other[:base]
        parts = exchange(chip, "space", 2)
        window = [pltpu.VMEM((3 * share, 24, TILE), F32), pltpu.VMEM((tiles + 1, 24, TILE), F32)]
        if step == 0:
            matrices, plan, near_part = call(
                functools.partial(pair_kernel, length_x, base, share),
                [((SLOTS, 2 * TILE, 6 * TILE), BF16), ((3, SLOTS), jnp.int32), rows_shape],
                (live, stack, rest, other, away),
                [pltpu.VMEM((tiles + 1, 8, TILE), F32), pltpu.VMEM((3 * share, TILE, 8), F32), *window],
                smem_in=1,
                smem_out=(1,),
                flops=20 * far_flops,
            )
        else:
            near_part = call(
                functools.partial(near_kernel, base, share),
                [rows_shape],
                (plan, rest, other, away, matrices),
                window,
                smem_in=1,
                flops=20 * far_flops,
            )[0]
        parts[-1], near_part = lax.optimization_barrier((parts[-1], near_part))
        total = functools.reduce(jnp.add, parts)
        swapped = lax.ppermute(total[:half], "space", core)
        part = near_part
        for begin, factors in ((0, total), (waves // 2, swapped)):
            part = call(
                functools.partial(back_kernel, begin),
                [rows_shape],
                (factors, part, terms, flipped),
                [pltpu.VMEM((2, 6 * vectors, waves // 2), BF16)],
                flops=far_flops // 2,
            )[0]
        norms.append(total)
        sums = exchange(part, "wave", 1)
        if step < DEGREE - 1:
            rows, own, norm = call(
                functools.partial(next_kernel, len(sums), share),
                [rows_shape, ((24 * share, TILE), F32), ((8, TILE), F32)],
                (*sums, rows, terms),
                flops=1,
            )
            mine, rest = call(
                factor_kernel,
                [((half, TILE), F32), ((base + 24 * share, TILE), F32)],
                (rows, own, norm, terms, phases),
                flops=far_flops,
            )
            images.append(rows)
    series, scale = call(
        series_kernel,
        [rows_shape, ((16, TILE), F32)],
        (noise_rows, *images, *norms[1:]),
        flops=5 * far_flops,
    )
    out = call(
        functools.partial(final_kernel, len(sums)),
        [rows_shape],
        (*sums, series, scale),
        flops=1,
    )[0]
    return jnp.transpose(out.reshape(3, vectors, particles), (1, 0, 2))


def solution(mesh):
    in_specs = (
        P(None, None, "space"),
        P(None, "space"),
        P(None, "wave"),
        P("space", None),
        P("space"),
    )
    out_specs = P(None, None, "space")
    return jax.shard_map(body, mesh=mesh, in_specs=in_specs, out_specs=out_specs, check_vma=False)
```

```python
import functools
import math

import jax
import jax.numpy as jnp
from jax import lax
from jax.experimental import pallas as pl
from jax.experimental.pallas import tpu as pltpu
from jax.sharding import PartitionSpec as P

TILE = 128
KW = 4096
NB_MOST = 8
DEGREE = 3
PAIR_MOST = 32
GROUP = 4
SLOTS = PAIR_MOST + GROUP

SIDE_CROSS = 8.0
NEAR_SQUARE = 0.36
NEAR_AMP = 0.15
FAR_AMP = 8.0
SPLIT_SQUARE = 64.0
SCREEN = 4.0
SAFETY = 1.25
SPREAD = 100.0
EPSILON = 1e-06

F32 = jnp.float32
BF16 = jnp.bfloat16
VMEM_LIMIT = 8 << 20

SINE = (4.44287968, -7.30781651, 3.59777427, -0.791199386)
ROUNDER = 12582912.0
COSINE = (1.4142040014266968, -6.97763729095459, 5.715188026428223, -1.728213906288147)


def split(x):
    high = x.astype(BF16)
    return high, (x - high.astype(F32)).astype(BF16)


def poly(coeffs, x):
    acc = coeffs[-1]
    for c in coeffs[-2::-1]:
        acc = acc * x + c
    return acc


def emit(kinds, terms, at, mine_ref, rest_ref):
    width = kinds[0].shape[1]
    t = terms[:, at : at + width]
    pieces = []
    for full in kinds:
        fx, fy, fz = full[0:8], full[8:16], full[16:24]
        pieces.append(t[1:2] * fx + t[2:3] * fy)
        pieces.append(t[3:4] * fx + t[4:5] * fy + t[5:6] * fz)
    stacked = jnp.concatenate(pieces, axis=0)
    half = mine_ref.shape[0]
    for k in range(width // TILE):
        row = (at // TILE + k) * 32
        ref, row = (mine_ref, row) if row < half else (rest_ref, row - half)
        ref[row : row + 32, :] = stacked[:, k * TILE : (k + 1) * TILE]


def product(both, high_table, low_table):
    first = jnp.dot(both, high_table, preferred_element_type=F32)
    second = jnp.dot(both[:24], low_table, preferred_element_type=F32)
    return first[:24] + (first[24:] + second)


def forward(rows, table_ref, terms, mine_ref, rest_ref):
    waves = table_ref.shape[2]
    both = jnp.concatenate(split(rows), axis=0)
    step = min(512, waves)
    for at in range(0, waves, step):
        cols = slice(at, at + step)
        kinds = [product(both, table_ref[k, :, cols], table_ref[2 + k, :, cols]) for k in range(2)]
        emit(kinds, terms, at, mine_ref, rest_ref)


def own_tiles(rows, share, rank, ranks):
    picked = []
    for k in range(share):
        tiles = [rows[:, t * TILE : (t + 1) * TILE] for t in range(k * ranks, (k + 1) * ranks)]
        mine = tiles[0]
        for r in range(1, ranks):
            mine = jnp.where(jnp.abs(rank - r) < 0.5, tiles[r], mine)
        picked.append(mine)
    return jnp.concatenate(picked, axis=0)


def start_kernel(
    length_x, share, index_ref, place_ref, stack_ref, table_ref, flip_ref, terms_ref, mine_ref, rest_ref,
    turn_ref, left_ref, sum_ref
):
    particles = table_ref.shape[1]
    waves = table_ref.shape[2]
    tiles = particles // TILE
    ranks = tiles // share
    sides = (length_x, SIDE_CROSS, SIDE_CROSS)
    core = place_ref[0:1]
    rank = place_ref[1:2]
    whole = index_ref[...].astype(F32)
    turned = jnp.concatenate([whole[:, waves // 2 :], whole[:, : waves // 2]], axis=1)
    first = jnp.broadcast_to(jnp.concatenate([core] * (waves // TILE), axis=1), whole.shape) < 0.5
    whole = jnp.where(first, whole, turned)
    counts = [whole[a : a + 1] for a in range(3)]
    k1, k2, k3 = [2.0 * math.pi * counts[a] / sides[a] for a in range(3)]
    square = k1 * k1 + k2 * k2 + k3 * k3
    scaled = square / SPLIT_SQUARE
    weight = FAR_AMP * (1.0 + scaled) * jnp.exp(-scaled) / (KW * (square + SCREEN))
    flat_square = k1 * k1 + k2 * k2
    flat = 1.0 / jnp.sqrt(flat_square)
    both = 1.0 / jnp.sqrt(square * flat_square)
    terms_ref[...] = jnp.concatenate(
        [
            weight,
            -k2 * flat,
            k1 * flat,
            -k1 * k3 * both,
            -k2 * k3 * both,
            flat_square * both,
            jnp.concatenate([place_ref[...]] * (waves // TILE), axis=1),
        ],
        axis=0,
    )
    noise = stack_ref[0:24, :particles]
    places = jnp.concatenate([stack_ref[24:27, :particles], jnp.zeros((5, particles), F32)], axis=0)
    base = waves // TILE * 16
    row = base + 8 + 24 * share
    rest_ref[base : base + 8, :] = jnp.zeros((8, TILE), F32)
    rest_ref[base + 8 : row, :] = own_tiles(noise, share, rank, ranks)
    rest_ref[row : row + 8 * share, :] = own_tiles(places, share, rank, ranks)
    left_ref[...] = jnp.concatenate(split(noise), axis=0)
    parts = []
    rest = jnp.concatenate([places[a : a + 1] / sides[a] for a in range(3)], axis=0)
    for _ in range(3):
        parts.append(rest.astype(BF16).astype(F32))
        rest = rest - parts[-1]
    turn_ref[...] = jnp.concatenate(parts + [jnp.zeros((7, particles), F32)], axis=0).T.astype(BF16)
    numbers = jnp.concatenate(counts * 3 + [jnp.zeros((7, waves), F32)], axis=0).astype(BF16)
    wide = 256

    def make(rows):
        for at in range(0, waves, wide):
            turns = jnp.dot(turn_ref[rows, :], numbers[:, at : at + wide], preferred_element_type=F32)
            for j in range(0, wide, TILE):
                cols = slice(at + j, at + j + TILE)
                t = turns[:, j : j + TILE]
                r = t - ((t + ROUNDER) - ROUNDER)
                x = r * r
                s = r * poly(SINE, x)
                c = poly(COSINE, x)
                table_ref[0, rows, cols], table_ref[2, rows, cols] = split(1.0 - s * s)
                table_ref[1, rows, cols], table_ref[3, rows, cols] = split(s * c)

    def use(rows, first):
        for kind in range(2):
            for at in range(0, waves, wide):
                cols = slice(at, at + wide)
                piece = product(left_ref[:, rows], table_ref[kind, rows, cols], table_ref[2 + kind, rows, cols])
                sum_ref[kind, :, cols] = piece if first else sum_ref[kind, :, cols] + piece
        for kind in range(4):
            flip_ref[kind, :, rows] = table_ref[kind, rows, :].T

    ends = [0] + [particles * k // 8 for k in (4, 7, 8)]
    blocks = [slice(low, high) for low, high in zip(ends, ends[1:])]
    make(blocks[0])
    for k in range(1, len(blocks)):
        use(blocks[k - 1], k == 1)
        make(blocks[k])
    use(blocks[-1], len(blocks) == 1)
    emit([sum_ref[0], sum_ref[1]], terms_ref[...], 0, mine_ref, rest_ref)


def fill_window(sources, share, window_ref):
    for slab, (ref, start) in enumerate(sources):
        for i in range(share):
            row = start + 24 * i
            window_ref[slab * share + i] = ref[row : row + 24, :]


def add_pair(target, source, matrix, sum_ref):
    high, low = split(source)
    left = jnp.concatenate(
        [
            jnp.concatenate([high, high], axis=1),
            jnp.concatenate([low, jnp.zeros_like(low)], axis=1),
        ],
        axis=0,
    )
    both = jnp.dot(left, matrix, preferred_element_type=F32)
    full = both[:24] + both[24:]
    x, y, z = full[0:8], full[8:16], full[16:24]

    def part(rows, at):
        return rows[:, at * TILE : (at + 1) * TILE]

    sum_ref[target] += jnp.concatenate(
        [
            part(x, 0) + part(y, 1) + part(z, 2),
            part(x, 1) + part(y, 3) + part(z, 4),
            part(x, 2) + part(y, 4) + part(z, 5),
        ],
        axis=0,
    )


def pair_kernel(
    length_x, base, share, live_ref, pos_ref, own_ref, near_ref, away_ref, out_ref, plan_ref, near_out_ref,
    place_ref, column_ref, window_ref, sum_ref
):
    tiles = pos_ref.shape[1] // TILE
    seen = jnp.int32(0)
    for target in range(tiles):
        for k in range(NB_MOST):
            code = live_ref[target, k]
            plan_ref[0, seen] = target
            plan_ref[1, seen] = code
            seen = seen + jnp.where(code >= 0, 1, 0)
    plan_ref[2, 0] = seen
    for k in range(GROUP):
        plan_ref[0, seen + k] = tiles
        plan_ref[1, seen + k] = 0
    fill_window(((own_ref, base), (near_ref, base), (away_ref, 0)), share, window_ref)
    sum_ref[...] = jnp.zeros_like(sum_ref)
    base = base + 24 * share
    sides = (length_x, SIDE_CROSS, SIDE_CROSS)
    reach = math.sqrt(NEAR_SQUARE)
    filler = jnp.zeros((5, TILE), F32)
    for i in range(tiles):
        lanes = slice(i * TILE, (i + 1) * TILE)
        place_ref[i] = jnp.concatenate([pos_ref[24 + a : 25 + a, lanes] / sides[a] for a in range(3)] + [filler], axis=0)
    for slab, ref in enumerate((own_ref, near_ref, away_ref)):
        for i in range(share):
            row = (base if slab < 2 else 24 * share) + 8 * i
            place = ref[row : row + 8, :]
            place = jnp.concatenate([place[a : a + 1] / sides[a] for a in range(3)] + [filler], axis=0)
            column_ref[slab * share + i] = place.T
    count = 32

    def pair(p, carry):
        q = jnp.maximum(p - 1, 0)
        add_pair(
            jnp.where(p == 0, tiles, plan_ref[0, q]), window_ref[plan_ref[1, q] >> 1], out_ref[q], sum_ref
        )
        target = place_ref[plan_ref[0, p]]
        source = column_ref[plan_ref[1, p] >> 1]
        own = (plan_ref[1, p] & 1).astype(F32)
        lines = [target[a : a + 1] for a in range(3)]
        for low in range(0, TILE, count):
            rows = slice(low, low + count)
            q = []
            for a in range(3):
                offset = lines[a] - jnp.broadcast_to(source[rows, a : a + 1], (count, TILE))
                offset = offset - jnp.floor(offset + 0.5)
                q.append(offset * (sides[a] / reach))
            square = q[0] * q[0] + q[1] * q[1] + q[2] * q[2]
            same = (
                lax.broadcasted_iota(jnp.int32, (count, TILE), 0) + low
                == lax.broadcasted_iota(jnp.int32, (count, TILE), 1)
            )
            envelope = jnp.exp(-square) * jnp.where(same, NEAR_AMP * (1.0 - own), NEAR_AMP)
            slot = 0
            for a in range(3):
                scaled = envelope * q[a]
                for b in range(a, 3):
                    value = scaled * q[b]
                    if a == b:
                        value = value + envelope
                    cols = slice(slot * TILE, (slot + 1) * TILE)
                    out_ref[p, rows, cols], out_ref[p, TILE + low : TILE + low + count, cols] = split(value)
                    slot += 1
        return carry

    lax.fori_loop(0, seen + 1, pair, 0)
    for i in range(tiles):
        near_out_ref[:, i * TILE : (i + 1) * TILE] = sum_ref[i]


def near_kernel(base, share, plan_ref, own_ref, near_ref, away_ref, matrix_ref, out_ref, window_ref, sum_ref):
    fill_window(((own_ref, base), (near_ref, base), (away_ref, 0)), share, window_ref)
    sum_ref[...] = jnp.zeros_like(sum_ref)

    def several(at, carry):
        for k in range(GROUP):
            p = at * GROUP + k
            add_pair(plan_ref[0, p], window_ref[plan_ref[1, p] >> 1], matrix_ref[p], sum_ref)
        return carry

    lax.fori_loop(0, lax.div(plan_ref[2, 0] + (GROUP - 1), GROUP), several, 0)
    for i in range(sum_ref.shape[0] - 1):
        out_ref[:, i * TILE : (i + 1) * TILE] = sum_ref[i]


def back_kernel(begin, factor_ref, before_ref, terms_ref, flip_ref, out_ref, left_ref):
    waves = left_ref.shape[2]
    particles = out_ref.shape[1]
    for i in range(waves // TILE):
        block = factor_ref[32 * i : 32 * i + 32, :]
        t = terms_ref[:, begin + i * TILE : begin + (i + 1) * TILE]
        block = block * t[0:1]
        for kind in range(2):
            one, two = block[16 * kind : 16 * kind + 8], block[16 * kind + 8 : 16 * kind + 16]
            rows = jnp.concatenate(
                [t[1:2] * one + t[3:4] * two, t[2:3] * one + t[4:5] * two, t[5:6] * two], axis=0
            )
            left_ref[kind, :, i * TILE : (i + 1) * TILE] = jnp.concatenate(split(rows), axis=0)
    step = min(512, particles)
    rows = slice(begin, begin + waves)
    for at in range(0, particles, step):
        cols = slice(at, at + step)
        total = before_ref[:, cols]
        for k in range(2):
            total = total + product(left_ref[k], flip_ref[k, rows, cols], flip_ref[2 + k, rows, cols])
        out_ref[:, cols] = total


def next_kernel(parts, share, *refs):
    ins, (force_ref, terms_ref, rows_ref, tiles_ref, norm_ref) = refs[:parts], refs[parts:]
    particles = force_ref.shape[1]
    total = ins[0][...]
    for ref in ins[1:]:
        total = total + ref[...]
    rows = force_ref[...] + total
    rows_ref[...] = rows
    tiles_ref[...] = own_tiles(rows, share, terms_ref[7:8, :TILE], particles // TILE // share)
    squares = rows * rows
    squares = squares[0:8] + squares[8:16] + squares[16:24]
    norm = squares[:, 0:TILE]
    for i in range(1, particles // TILE):
        norm = norm + squares[:, i * TILE : (i + 1) * TILE]
    norm_ref[...] = norm


def factor_kernel(rows_ref, tiles_ref, norm_ref, terms_ref, table_ref, mine_ref, rest_ref):
    base = mine_ref.shape[0]
    rest_ref[base : base + 8, :] = norm_ref[...]
    rest_ref[base + 8 :, :] = tiles_ref[...]
    forward(rows_ref[...], table_ref, terms_ref[...], mine_ref, rest_ref)


def series_kernel(noise_ref, one_ref, two_ref, first_ref, second_ref, base_ref, scale_ref):
    u0, u1, u2 = noise_ref[...], one_ref[...], two_ref[...]
    first = jnp.sum(first_ref[-8:, :], axis=1, keepdims=True)
    second = jnp.sum(second_ref[-8:, :], axis=1, keepdims=True)
    ratio = jnp.max(second / (first + EPSILON), axis=0, keepdims=True)
    high = SAFETY * jnp.sqrt(ratio)
    low = high / SPREAD
    nodes = DEGREE + 1
    angles = [math.pi * (j + 0.5) / nodes for j in range(nodes)]
    samples = [jnp.sqrt(0.5 * (high - low) * math.cos(t) + 0.5 * (high + low)) for t in angles]
    coeffs = []
    for k in range(nodes):
        acc = samples[0] * math.cos(k * angles[0])
        for j in range(1, nodes):
            acc = acc + samples[j] * math.cos(k * angles[j])
        coeffs.append(acc * (2.0 / nodes) * (0.5 if k == 0 else 1.0))
    p = 2.0 / (high - low)
    q = (high + low) / (high - low)
    v0, v1, v2 = p * u1 - q * u0, p * u2 - q * u1, p * u2 - q * u2
    t2 = 2.0 * (p * v1 - q * v0) - u0
    m2 = 2.0 * (p * v2 - q * v1) - u1
    t3 = 2.0 * (p * m2 - q * t2) - v0
    base_ref[...] = coeffs[0] * u0 + coeffs[1] * v0 + coeffs[2] * t2 + coeffs[3] * t3
    scale_ref[0:8, :] = jnp.broadcast_to(p, (8, TILE))
    scale_ref[8:16, :] = jnp.broadcast_to(coeffs[3], (8, TILE))


def final_kernel(parts, *refs):
    ins, (base_ref, scale_ref, out_ref) = refs[:parts], refs[parts:]
    total = ins[0][...]
    for ref in ins[1:]:
        total = total + ref[...]
    p, last = scale_ref[0:1, 0:1], scale_ref[8:9, 0:1]
    out_ref[...] = base_ref[...] + last * (2.0 * p * (2.0 * p * (p * total)))


def call(kernel, outs, args, scratch=(), smem_in=0, smem_out=(), flops=0, space=pltpu.VMEM):
    vmem = pl.BlockSpec(memory_space=pltpu.VMEM)
    smem = pl.BlockSpec(memory_space=pltpu.SMEM)
    return pl.pallas_call(
        kernel,
        out_shape=[jax.ShapeDtypeStruct(*o) for o in outs],
        in_specs=[smem] * smem_in + [pl.BlockSpec(memory_space=space)] * (len(args) - smem_in),
        out_specs=[smem if i in smem_out else vmem for i in range(len(outs))],
        scratch_shapes=list(scratch),
        cost_estimate=pl.CostEstimate(flops=flops, bytes_accessed=0, transcendentals=0),
        compiler_params=pltpu.CompilerParams(vmem_limit_bytes=VMEM_LIMIT),
    )(*args)


def exchange(x, axis, lowest):
    size = lax.axis_size(axis)
    bit = lowest
    parts = [x]
    while bit < size:
        if len(parts) > 1:
            x = functools.reduce(jnp.add, parts)
        radix = min(4, size // bit)
        parts = [x] + [
            lax.ppermute(x, axis, [(i, i ^ (d * bit)) for i in range(size)]) for d in ((2, 1, 3) if radix == 4 else range(1, radix))
        ]
        bit *= radix
    return parts


def body(noise, positions, wave_index, tile_lists, tile_counts):
    slabs = lax.axis_size("space")
    length_x = float(slabs)
    vectors = noise.shape[0]
    particles = positions.shape[1]
    waves = wave_index.shape[1]
    tiles = particles // TILE
    ranks = lax.axis_size("wave")
    share = tiles // ranks
    place = jnp.stack([lax.axis_index("space") & 1, lax.axis_index("wave")]).astype(jnp.int32)
    core = [(i, i ^ 1) for i in range(slabs)]
    third = [(i, (i + 1 if i % 2 else i - 1) % slabs) for i in range(slabs)]
    table = ((4, particles, waves), BF16)
    rows_shape = ((3 * vectors, particles), F32)
    half = waves // TILE * 16
    base = half + 8
    far_flops = 2 * 96 * particles * waves * 2

    rows = jnp.transpose(noise, (1, 0, 2)).reshape(3 * vectors, particles)
    lines = jnp.broadcast_to(place.astype(F32)[:, None], (2, TILE))
    stack = jnp.concatenate([rows, positions], axis=0)
    phases, flipped, terms, mine, rest = call(
        functools.partial(start_kernel, length_x, share),
        [
            table,
            ((4, waves, particles), BF16),
            ((8, waves), F32),
            ((half, TILE), F32),
            ((base + 32 * share, TILE), F32),
        ],
        (wave_index, lines, stack),
        [
            pltpu.VMEM((particles, 16), BF16),
            pltpu.VMEM((6 * vectors, particles), BF16),
            pltpu.VMEM((2, 3 * vectors, waves), F32),
        ],
        flops=4 * far_flops,
    )
    core_line = jnp.broadcast_to(terms[6:7, :NB_MOST], tile_lists.shape)
    rank_line = jnp.broadcast_to(terms[7:8, :NB_MOST], tile_lists.shape)
    side, tile = tile_lists // tiles, tile_lists % tiles
    which = jnp.where(side == 1, 0, jnp.where((side == 0) == (core_line > 0.5), 1, 2))
    targets = lax.broadcasted_iota(jnp.int32, tile_lists.shape, 0)
    slots = lax.broadcasted_iota(jnp.int32, tile_lists.shape, 1)
    itself = tile_lists - targets == tiles
    code = 2 * (which * share + tile // ranks) + itself.astype(jnp.int32)
    wanted = (slots < tile_counts[:, None]) & (tile % ranks == rank_line.astype(jnp.int32))
    live = jnp.where(wanted, code, -1)
    noise_rows = rows
    images, norms = [], []

    matrices = plan = None
    for step in range(DEGREE):
        other = lax.ppermute(rest, "space", core)
        away = lax.ppermute(rest[base:] if step == 0 else own, "space", third)
        if step == 0:
            other, live = lax.optimization_barrier((other, live))
        chip = jnp.concatenate([mine, rest[half:base]], axis=0) + other[:base]
        parts = exchange(chip, "space", 2)
        window = [pltpu.VMEM((3 * share, 24, TILE), F32), pltpu.VMEM((tiles + 1, 24, TILE), F32)]
        if step == 0:
            matrices, plan, near_part = call(
                functools.partial(pair_kernel, length_x, base, share),
                [((SLOTS, 2 * TILE, 6 * TILE), BF16), ((3, SLOTS), jnp.int32), rows_shape],
                (live, stack, rest, other, away),
                [pltpu.VMEM((tiles + 1, 8, TILE), F32), pltpu.VMEM((3 * share, TILE, 8), F32), *window],
                smem_in=1,
                smem_out=(1,),
                flops=20 * far_flops,
            )
        else:
            near_part = call(
                functools.partial(near_kernel, base, share),
                [rows_shape],
                (plan, rest, other, away, matrices),
                window,
                smem_in=1,
                flops=20 * far_flops,
            )[0]
        parts[-1], near_part = lax.optimization_barrier((parts[-1], near_part))
        total = functools.reduce(jnp.add, parts)
        swapped = lax.ppermute(total[:half], "space", core)
        part = near_part
        for begin, factors in ((0, total), (waves // 2, swapped)):
            part = call(
                functools.partial(back_kernel, begin),
                [rows_shape],
                (factors, part, terms, flipped),
                [pltpu.VMEM((2, 6 * vectors, waves // 2), BF16)],
                flops=far_flops // 2,
            )[0]
        norms.append(total)
        sums = exchange(part, "wave", 1)
        if step < DEGREE - 1:
            rows, own, norm = call(
                functools.partial(next_kernel, len(sums), share),
                [rows_shape, ((24 * share, TILE), F32), ((8, TILE), F32)],
                (*sums, rows, terms),
                flops=1,
            )
            mine, rest = call(
                factor_kernel,
                [((half, TILE), F32), ((base + 24 * share, TILE), F32)],
                (rows, own, norm, terms, phases),
                flops=far_flops,
            )
            images.append(rows)
    series, scale = call(
        series_kernel,
        [rows_shape, ((16, TILE), F32)],
        (noise_rows, *images, *norms[1:]),
        flops=5 * far_flops,
    )
    out = call(
        functools.partial(final_kernel, len(sums)),
        [rows_shape],
        (*sums, series, scale),
        flops=1,
    )[0]
    return jnp.transpose(out.reshape(3, vectors, particles), (1, 0, 2))


def solution(mesh):
    in_specs = (
        P(None, None, "space"),
        P(None, "space"),
        P(None, "wave"),
        P("space", None),
        P("space"),
    )
    out_specs = P(None, None, "space")
    return jax.shard_map(body, mesh=mesh, in_specs=in_specs, out_specs=out_specs, check_vma=False)
```

```python
import functools
import math

import jax
import jax.numpy as jnp
from jax import lax
from jax.experimental import pallas as pl
from jax.experimental.pallas import tpu as pltpu
from jax.sharding import PartitionSpec as P

TILE = 128
KW = 4096
NB_MOST = 8
DEGREE = 3
PAIR_MOST = 32
GROUP = 4
SLOTS = PAIR_MOST + GROUP

SIDE_CROSS = 8.0
NEAR_SQUARE = 0.36
NEAR_AMP = 0.15
FAR_AMP = 8.0
SPLIT_SQUARE = 64.0
SCREEN = 4.0
SAFETY = 1.25
SPREAD = 100.0
EPSILON = 1e-06

F32 = jnp.float32
BF16 = jnp.bfloat16
VMEM_LIMIT = 8 << 20

SINE = (4.44287968, -7.30781651, 3.59777427, -0.791199386)
ROUNDER = 12582912.0
COSINE = (1.4142040014266968, -6.97763729095459, 5.715188026428223, -1.728213906288147)


def split(x):
    high = x.astype(BF16)
    return high, (x - high.astype(F32)).astype(BF16)


def poly(coeffs, x):
    acc = coeffs[-1]
    for c in coeffs[-2::-1]:
        acc = acc * x + c
    return acc


def emit(kinds, terms, at, mine_ref, rest_ref):
    width = kinds[0].shape[1]
    t = terms[:, at : at + width]
    pieces = []
    for full in kinds:
        fx, fy, fz = full[0:8], full[8:16], full[16:24]
        pieces.append(t[1:2] * fx + t[2:3] * fy)
        pieces.append(t[3:4] * fx + t[4:5] * fy + t[5:6] * fz)
    stacked = jnp.concatenate(pieces, axis=0)
    half = mine_ref.shape[0]
    for k in range(width // TILE):
        row = (at // TILE + k) * 32
        ref, row = (mine_ref, row) if row < half else (rest_ref, row - half)
        ref[row : row + 32, :] = stacked[:, k * TILE : (k + 1) * TILE]


def product(both, high_table, low_table):
    first = jnp.dot(both, high_table, preferred_element_type=F32)
    second = jnp.dot(both[:24], low_table, preferred_element_type=F32)
    return first[:24] + (first[24:] + second)


def forward(rows, table_ref, terms, mine_ref, rest_ref):
    waves = table_ref.shape[2]
    both = jnp.concatenate(split(rows), axis=0)
    step = min(512, waves)
    for at in range(0, waves, step):
        cols = slice(at, at + step)
        kinds = [product(both, table_ref[k, :, cols], table_ref[2 + k, :, cols]) for k in range(2)]
        emit(kinds, terms, at, mine_ref, rest_ref)


def own_tiles(rows, share, rank, ranks):
    picked = []
    for k in range(share):
        tiles = [rows[:, t * TILE : (t + 1) * TILE] for t in range(k * ranks, (k + 1) * ranks)]
        mine = tiles[0]
        for r in range(1, ranks):
            mine = jnp.where(jnp.abs(rank - r) < 0.5, tiles[r], mine)
        picked.append(mine)
    return jnp.concatenate(picked, axis=0)


def start_kernel(
    length_x, share, index_ref, place_ref, stack_ref, table_ref, flip_ref, terms_ref, mine_ref, rest_ref,
    turn_ref, left_ref, sum_ref
):
    particles = table_ref.shape[1]
    waves = table_ref.shape[2]
    tiles = particles // TILE
    ranks = tiles // share
    sides = (length_x, SIDE_CROSS, SIDE_CROSS)
    core = place_ref[0:1]
    rank = place_ref[1:2]
    whole = index_ref[...].astype(F32)
    turned = jnp.concatenate([whole[:, waves // 2 :], whole[:, : waves // 2]], axis=1)
    first = jnp.broadcast_to(jnp.concatenate([core] * (waves // TILE), axis=1), whole.shape) < 0.5
    whole = jnp.where(first, whole, turned)
    counts = [whole[a : a + 1] for a in range(3)]
    k1, k2, k3 = [2.0 * math.pi * counts[a] / sides[a] for a in range(3)]
    square = k1 * k1 + k2 * k2 + k3 * k3
    scaled = square / SPLIT_SQUARE
    weight = FAR_AMP * (1.0 + scaled) * jnp.exp(-scaled) / (KW * (square + SCREEN))
    flat_square = k1 * k1 + k2 * k2
    flat = 1.0 / jnp.sqrt(flat_square)
    both = 1.0 / jnp.sqrt(square * flat_square)
    terms_ref[...] = jnp.concatenate(
        [
            weight,
            -k2 * flat,
            k1 * flat,
            -k1 * k3 * both,
            -k2 * k3 * both,
            flat_square * both,
            jnp.concatenate([place_ref[...]] * (waves // TILE), axis=1),
        ],
        axis=0,
    )
    noise = stack_ref[0:24, :particles]
    places = jnp.concatenate([stack_ref[24:27, :particles], jnp.zeros((5, particles), F32)], axis=0)
    base = waves // TILE * 16
    row = base + 8 + 24 * share
    rest_ref[base : base + 8, :] = jnp.zeros((8, TILE), F32)
    rest_ref[base + 8 : row, :] = own_tiles(noise, share, rank, ranks)
    rest_ref[row : row + 8 * share, :] = own_tiles(places, share, rank, ranks)
    left_ref[...] = jnp.concatenate(split(noise), axis=0)
    parts = []
    rest = jnp.concatenate([places[a : a + 1] / sides[a] for a in range(3)], axis=0)
    for _ in range(3):
        parts.append(rest.astype(BF16).astype(F32))
        rest = rest - parts[-1]
    turn_ref[...] = jnp.concatenate(parts + [jnp.zeros((7, particles), F32)], axis=0).T.astype(BF16)
    numbers = jnp.concatenate(counts * 3 + [jnp.zeros((7, waves), F32)], axis=0).astype(BF16)
    wide = 256

    def make(rows):
        for at in range(0, waves, wide):
            turns = jnp.dot(turn_ref[rows, :], numbers[:, at : at + wide], preferred_element_type=F32)
            for j in range(0, wide, TILE):
                cols = slice(at + j, at + j + TILE)
                t = turns[:, j : j + TILE]
                r = t - ((t + ROUNDER) - ROUNDER)
                x = r * r
                s = r * poly(SINE, x)
                c = poly(COSINE, x)
                table_ref[0, rows, cols], table_ref[2, rows, cols] = split(1.0 - s * s)
                table_ref[1, rows, cols], table_ref[3, rows, cols] = split(s * c)

    def use(rows, first):
        for kind in range(2):
            for at in range(0, waves, wide):
                cols = slice(at, at + wide)
                piece = product(left_ref[:, rows], table_ref[kind, rows, cols], table_ref[2 + kind, rows, cols])
                sum_ref[kind, :, cols] = piece if first else sum_ref[kind, :, cols] + piece
        for kind in range(4):
            flip_ref[kind, :, rows] = table_ref[kind, rows, :].T

    ends = [0] + [particles * k // 8 for k in (4, 7, 8)]
    blocks = [slice(low, high) for low, high in zip(ends, ends[1:])]
    make(blocks[0])
    for k in range(1, len(blocks)):
        use(blocks[k - 1], k == 1)
        make(blocks[k])
    use(blocks[-1], len(blocks) == 1)
    emit([sum_ref[0], sum_ref[1]], terms_ref[...], 0, mine_ref, rest_ref)


def fill_window(sources, share, window_ref):
    for slab, (ref, start) in enumerate(sources):
        for i in range(share):
            row = start + 24 * i
            window_ref[slab * share + i] = ref[row : row + 24, :]


def add_pair(target, source, matrix, sum_ref):
    high, low = split(source)
    left = jnp.concatenate(
        [
            jnp.concatenate([high, high], axis=1),
            jnp.concatenate([low, jnp.zeros_like(low)], axis=1),
        ],
        axis=0,
    )
    both = jnp.dot(left, matrix, preferred_element_type=F32)
    full = both[:24] + both[24:]
    x, y, z = full[0:8], full[8:16], full[16:24]

    def part(rows, at):
        return rows[:, at * TILE : (at + 1) * TILE]

    sum_ref[target] += jnp.concatenate(
        [
            part(x, 0) + part(y, 1) + part(z, 2),
            part(x, 1) + part(y, 3) + part(z, 4),
            part(x, 2) + part(y, 4) + part(z, 5),
        ],
        axis=0,
    )


def pair_kernel(
    length_x, base, share, live_ref, pos_ref, own_ref, near_ref, away_ref, out_ref, plan_ref, near_out_ref,
    place_ref, column_ref, window_ref, sum_ref
):
    tiles = pos_ref.shape[1] // TILE
    seen = jnp.int32(0)
    for target in range(tiles):
        for k in range(NB_MOST):
            code = live_ref[target, k]
            plan_ref[0, seen] = target
            plan_ref[1, seen] = code
            seen = seen + jnp.where(code >= 0, 1, 0)
    plan_ref[2, 0] = seen
    for k in range(GROUP):
        plan_ref[0, seen + k] = tiles
        plan_ref[1, seen + k] = 0
    fill_window(((own_ref, base), (near_ref, base), (away_ref, 0)), share, window_ref)
    sum_ref[...] = jnp.zeros_like(sum_ref)
    base = base + 24 * share
    sides = (length_x, SIDE_CROSS, SIDE_CROSS)
    reach = math.sqrt(NEAR_SQUARE)
    filler = jnp.zeros((5, TILE), F32)
    for i in range(tiles):
        lanes = slice(i * TILE, (i + 1) * TILE)
        place_ref[i] = jnp.concatenate([pos_ref[24 + a : 25 + a, lanes] / sides[a] for a in range(3)] + [filler], axis=0)
    for slab, ref in enumerate((own_ref, near_ref, away_ref)):
        for i in range(share):
            row = (base if slab < 2 else 24 * share) + 8 * i
            place = ref[row : row + 8, :]
            place = jnp.concatenate([place[a : a + 1] / sides[a] for a in range(3)] + [filler], axis=0)
            column_ref[slab * share + i] = place.T
    count = 64

    def pair(p, carry):
        q = jnp.maximum(p - 1, 0)
        add_pair(
            jnp.where(p == 0, tiles, plan_ref[0, q]), window_ref[plan_ref[1, q] >> 1], out_ref[q], sum_ref
        )
        target = place_ref[plan_ref[0, p]]
        source = column_ref[plan_ref[1, p] >> 1]
        own = (plan_ref[1, p] & 1).astype(F32)
        lines = [target[a : a + 1] for a in range(3)]
        for low in range(0, TILE, count):
            rows = slice(low, low + count)
            q = []
            for a in range(3):
                offset = lines[a] - jnp.broadcast_to(source[rows, a : a + 1], (count, TILE))
                offset = offset - jnp.floor(offset + 0.5)
                q.append(offset * (sides[a] / reach))
            square = q[0] * q[0] + q[1] * q[1] + q[2] * q[2]
            same = (
                lax.broadcasted_iota(jnp.int32, (count, TILE), 0) + low
                == lax.broadcasted_iota(jnp.int32, (count, TILE), 1)
            )
            envelope = jnp.exp(-square) * jnp.where(same, NEAR_AMP * (1.0 - own), NEAR_AMP)
            slot = 0
            for a in range(3):
                scaled = envelope * q[a]
                for b in range(a, 3):
                    value = scaled * q[b]
                    if a == b:
                        value = value + envelope
                    cols = slice(slot * TILE, (slot + 1) * TILE)
                    out_ref[p, rows, cols], out_ref[p, TILE + low : TILE + low + count, cols] = split(value)
                    slot += 1
        return carry

    lax.fori_loop(0, seen + 1, pair, 0)
    for i in range(tiles):
        near_out_ref[:, i * TILE : (i + 1) * TILE] = sum_ref[i]


def near_kernel(base, share, plan_ref, own_ref, near_ref, away_ref, matrix_ref, out_ref, window_ref, sum_ref):
    fill_window(((own_ref, base), (near_ref, base), (away_ref, 0)), share, window_ref)
    sum_ref[...] = jnp.zeros_like(sum_ref)

    def several(at, carry):
        for k in range(GROUP):
            p = at * GROUP + k
            add_pair(plan_ref[0, p], window_ref[plan_ref[1, p] >> 1], matrix_ref[p], sum_ref)
        return carry

    lax.fori_loop(0, lax.div(plan_ref[2, 0] + (GROUP - 1), GROUP), several, 0)
    for i in range(sum_ref.shape[0] - 1):
        out_ref[:, i * TILE : (i + 1) * TILE] = sum_ref[i]


def back_kernel(begin, factor_ref, before_ref, terms_ref, flip_ref, out_ref, left_ref):
    waves = left_ref.shape[2]
    particles = out_ref.shape[1]
    for i in range(waves // TILE):
        block = factor_ref[32 * i : 32 * i + 32, :]
        t = terms_ref[:, begin + i * TILE : begin + (i + 1) * TILE]
        block = block * t[0:1]
        for kind in range(2):
            one, two = block[16 * kind : 16 * kind + 8], block[16 * kind + 8 : 16 * kind + 16]
            rows = jnp.concatenate(
                [t[1:2] * one + t[3:4] * two, t[2:3] * one + t[4:5] * two, t[5:6] * two], axis=0
            )
            left_ref[kind, :, i * TILE : (i + 1) * TILE] = jnp.concatenate(split(rows), axis=0)
    step = min(512, particles)
    rows = slice(begin, begin + waves)
    for at in range(0, particles, step):
        cols = slice(at, at + step)
        total = before_ref[:, cols]
        for k in range(2):
            total = total + product(left_ref[k], flip_ref[k, rows, cols], flip_ref[2 + k, rows, cols])
        out_ref[:, cols] = total


def next_kernel(parts, share, *refs):
    ins, (force_ref, terms_ref, rows_ref, tiles_ref, norm_ref) = refs[:parts], refs[parts:]
    particles = force_ref.shape[1]
    total = ins[0][...]
    for ref in ins[1:]:
        total = total + ref[...]
    rows = force_ref[...] + total
    rows_ref[...] = rows
    tiles_ref[...] = own_tiles(rows, share, terms_ref[7:8, :TILE], particles // TILE // share)
    squares = rows * rows
    squares = squares[0:8] + squares[8:16] + squares[16:24]
    norm = squares[:, 0:TILE]
    for i in range(1, particles // TILE):
        norm = norm + squares[:, i * TILE : (i + 1) * TILE]
    norm_ref[...] = norm


def factor_kernel(rows_ref, tiles_ref, norm_ref, terms_ref, table_ref, mine_ref, rest_ref):
    base = mine_ref.shape[0]
    rest_ref[base : base + 8, :] = norm_ref[...]
    rest_ref[base + 8 :, :] = tiles_ref[...]
    forward(rows_ref[...], table_ref, terms_ref[...], mine_ref, rest_ref)


def series_kernel(noise_ref, one_ref, two_ref, first_ref, second_ref, base_ref, scale_ref):
    u0, u1, u2 = noise_ref[...], one_ref[...], two_ref[...]
    first = jnp.sum(first_ref[-8:, :], axis=1, keepdims=True)
    second = jnp.sum(second_ref[-8:, :], axis=1, keepdims=True)
    ratio = jnp.max(second / (first + EPSILON), axis=0, keepdims=True)
    high = SAFETY * jnp.sqrt(ratio)
    low = high / SPREAD
    nodes = DEGREE + 1
    angles = [math.pi * (j + 0.5) / nodes for j in range(nodes)]
    samples = [jnp.sqrt(0.5 * (high - low) * math.cos(t) + 0.5 * (high + low)) for t in angles]
    coeffs = []
    for k in range(nodes):
        acc = samples[0] * math.cos(k * angles[0])
        for j in range(1, nodes):
            acc = acc + samples[j] * math.cos(k * angles[j])
        coeffs.append(acc * (2.0 / nodes) * (0.5 if k == 0 else 1.0))
    p = 2.0 / (high - low)
    q = (high + low) / (high - low)
    v0, v1, v2 = p * u1 - q * u0, p * u2 - q * u1, p * u2 - q * u2
    t2 = 2.0 * (p * v1 - q * v0) - u0
    m2 = 2.0 * (p * v2 - q * v1) - u1
    t3 = 2.0 * (p * m2 - q * t2) - v0
    base_ref[...] = coeffs[0] * u0 + coeffs[1] * v0 + coeffs[2] * t2 + coeffs[3] * t3
    scale_ref[0:8, :] = jnp.broadcast_to(p, (8, TILE))
    scale_ref[8:16, :] = jnp.broadcast_to(coeffs[3], (8, TILE))


def final_kernel(parts, *refs):
    ins, (base_ref, scale_ref, out_ref) = refs[:parts], refs[parts:]
    total = ins[0][...]
    for ref in ins[1:]:
        total = total + ref[...]
    p, last = scale_ref[0:1, 0:1], scale_ref[8:9, 0:1]
    out_ref[...] = base_ref[...] + last * (2.0 * p * (2.0 * p * (p * total)))


def call(kernel, outs, args, scratch=(), smem_in=0, smem_out=(), flops=0, space=pltpu.VMEM):
    vmem = pl.BlockSpec(memory_space=pltpu.VMEM)
    smem = pl.BlockSpec(memory_space=pltpu.SMEM)
    return pl.pallas_call(
        kernel,
        out_shape=[jax.ShapeDtypeStruct(*o) for o in outs],
        in_specs=[smem] * smem_in + [pl.BlockSpec(memory_space=space)] * (len(args) - smem_in),
        out_specs=[smem if i in smem_out else vmem for i in range(len(outs))],
        scratch_shapes=list(scratch),
        cost_estimate=pl.CostEstimate(flops=flops, bytes_accessed=0, transcendentals=0),
        compiler_params=pltpu.CompilerParams(vmem_limit_bytes=VMEM_LIMIT),
    )(*args)


def exchange(x, axis, lowest):
    size = lax.axis_size(axis)
    bit = lowest
    parts = [x]
    while bit < size:
        if len(parts) > 1:
            x = functools.reduce(jnp.add, parts)
        radix = min(4, size // bit)
        parts = [x] + [
            lax.ppermute(x, axis, [(i, i ^ (d * bit)) for i in range(size)]) for d in ((2, 1, 3) if radix == 4 else range(1, radix))
        ]
        bit *= radix
    return parts


def body(noise, positions, wave_index, tile_lists, tile_counts):
    slabs = lax.axis_size("space")
    length_x = float(slabs)
    vectors = noise.shape[0]
    particles = positions.shape[1]
    waves = wave_index.shape[1]
    tiles = particles // TILE
    ranks = lax.axis_size("wave")
    share = tiles // ranks
    place = jnp.stack([lax.axis_index("space") & 1, lax.axis_index("wave")]).astype(jnp.int32)
    core = [(i, i ^ 1) for i in range(slabs)]
    third = [(i, (i + 1 if i % 2 else i - 1) % slabs) for i in range(slabs)]
    table = ((4, particles, waves), BF16)
    rows_shape = ((3 * vectors, particles), F32)
    half = waves // TILE * 16
    base = half + 8
    far_flops = 2 * 96 * particles * waves * 2

    rows = jnp.transpose(noise, (1, 0, 2)).reshape(3 * vectors, particles)
    lines = jnp.broadcast_to(place.astype(F32)[:, None], (2, TILE))
    stack = jnp.concatenate([rows, positions], axis=0)
    phases, flipped, terms, mine, rest = call(
        functools.partial(start_kernel, length_x, share),
        [
            table,
            ((4, waves, particles), BF16),
            ((8, waves), F32),
            ((half, TILE), F32),
            ((base + 32 * share, TILE), F32),
        ],
        (wave_index, lines, stack),
        [
            pltpu.VMEM((particles, 16), BF16),
            pltpu.VMEM((6 * vectors, particles), BF16),
            pltpu.VMEM((2, 3 * vectors, waves), F32),
        ],
        flops=4 * far_flops,
    )
    core_line = jnp.broadcast_to(terms[6:7, :NB_MOST], tile_lists.shape)
    rank_line = jnp.broadcast_to(terms[7:8, :NB_MOST], tile_lists.shape)
    side, tile = tile_lists // tiles, tile_lists % tiles
    which = jnp.where(side == 1, 0, jnp.where((side == 0) == (core_line > 0.5), 1, 2))
    targets = lax.broadcasted_iota(jnp.int32, tile_lists.shape, 0)
    slots = lax.broadcasted_iota(jnp.int32, tile_lists.shape, 1)
    itself = tile_lists - targets == tiles
    code = 2 * (which * share + tile // ranks) + itself.astype(jnp.int32)
    wanted = (slots < tile_counts[:, None]) & (tile % ranks == rank_line.astype(jnp.int32))
    live = jnp.where(wanted, code, -1)
    noise_rows = rows
    images, norms = [], []

    matrices = plan = None
    for step in range(DEGREE):
        other = lax.ppermute(rest, "space", core)
        away = lax.ppermute(rest[base:] if step == 0 else own, "space", third)
        if step == 0:
            other, live = lax.optimization_barrier((other, live))
        chip = jnp.concatenate([mine, rest[half:base]], axis=0) + other[:base]
        parts = exchange(chip, "space", 2)
        window = [pltpu.VMEM((3 * share, 24, TILE), F32), pltpu.VMEM((tiles + 1, 24, TILE), F32)]
        if step == 0:
            matrices, plan, near_part = call(
                functools.partial(pair_kernel, length_x, base, share),
                [((SLOTS, 2 * TILE, 6 * TILE), BF16), ((3, SLOTS), jnp.int32), rows_shape],
                (live, stack, rest, other, away),
                [pltpu.VMEM((tiles + 1, 8, TILE), F32), pltpu.VMEM((3 * share, TILE, 8), F32), *window],
                smem_in=1,
                smem_out=(1,),
                flops=20 * far_flops,
            )
        else:
            near_part = call(
                functools.partial(near_kernel, base, share),
                [rows_shape],
                (plan, rest, other, away, matrices),
                window,
                smem_in=1,
                flops=20 * far_flops,
            )[0]
        parts[-1], near_part = lax.optimization_barrier((parts[-1], near_part))
        total = functools.reduce(jnp.add, parts)
        swapped = lax.ppermute(total[:half], "space", core)
        part = near_part
        for begin, factors in ((0, total), (waves // 2, swapped)):
            part = call(
                functools.partial(back_kernel, begin),
                [rows_shape],
                (factors, part, terms, flipped),
                [pltpu.VMEM((2, 6 * vectors, waves // 2), BF16)],
                flops=far_flops // 2,
            )[0]
        norms.append(total)
        sums = exchange(part, "wave", 1)
        if step < DEGREE - 1:
            rows, own, norm = call(
                functools.partial(next_kernel, len(sums), share),
                [rows_shape, ((24 * share, TILE), F32), ((8, TILE), F32)],
                (*sums, rows, terms),
                flops=1,
            )
            mine, rest = call(
                factor_kernel,
                [((half, TILE), F32), ((base + 24 * share, TILE), F32)],
                (rows, own, norm, terms, phases),
                flops=far_flops,
            )
            images.append(rows)
    series, scale = call(
        series_kernel,
        [rows_shape, ((16, TILE), F32)],
        (noise_rows, *images, *norms[1:]),
        flops=5 * far_flops,
    )
    out = call(
        functools.partial(final_kernel, len(sums)),
        [rows_shape],
        (*sums, series, scale),
        flops=1,
    )[0]
    return jnp.transpose(out.reshape(3, vectors, particles), (1, 0, 2))


def solution(mesh):
    in_specs = (
        P(None, None, "space"),
        P(None, "space"),
        P(None, "wave"),
        P("space", None),
        P("space"),
    )
    out_specs = P(None, None, "space")
    return jax.shard_map(body, mesh=mesh, in_specs=in_specs, out_specs=out_specs, check_vma=False)
```
